128 devices in a mesh: front: 64 (over z, y, x), panel: 2 (over core).
Axes of the slice: x: 4, y: 4, z: 4, core: 2. Of those that a mesh axis runs over, the one named last changes fastest.
Arguments:
- sep_factor: bfloat16 [65536, 1024], P(('front', 'panel')), may hold values from -3 to 3, as said below
- coup_factor: bfloat16 [131072, 1024], P(('front', 'panel')), may hold values from -0.1875 to 0.1875
- coup_list: int32 [64, 16], replicated, may hold values from -1 to 15, as said below
- slot_tiles: int32 [64, 16], replicated, may hold values from 0 to 1023, as said below
- anc_tiles: bfloat16 [32768, 128], P('front'), may hold values from -50 to 50
Outputs:
- selected_inverse: float32 [65536, 1024], P(('front', 'panel'))
- variances: float32 [65536], P(('front', 'panel'))
The draws below stay inside these ranges and needn't reach their ends.
Inputs may be any that keep to these rules, and one draw needn't show every extreme that they name: `sep_factor`: each front's block of 1024 rows is lower triangular with a diagonal of 1 or more. `coup_list`: a front's entries name distinct blocks; live entries come first and the rest are -1; every front has 4 or more live entries and some front has 16. `slot_tiles`: every strip id of 0 to 1023 appears in exactly one slot; every group holds exactly one strip of each block row.
All inputs are finite; a program needn't handle non-finite values.
Results may differ from the reference program's by a relative error of at most 0.0056.
Values may be sent and summed in bfloat16 or wider, within the bound.
No kernel may reach another device: no remote copies, remote signals or barrier semaphores. Data moves between devices by JAX's collectives and lax.ppermute only.
A program may use at most 128 MiB of HBM per device.

```python
import math
import jax
import jax.numpy as jnp
from jax import lax

NS = 1024
BLK = 128
MAXB = 16
NAB = 16
MAXA = 2048
STRIPS = 4
SR = 32
N_FRONT = 64


def slot_layout(key):
    keys = jax.random.split(key, 2)
    strip_count = NAB * N_FRONT
    row_keys = jax.random.split(keys[0], NAB)
    owner = jax.vmap(lambda row_key: jax.random.permutation(row_key, N_FRONT))(row_keys).reshape(-1)
    jitter = jax.random.permutation(keys[1], strip_count)
    order = jnp.argsort(owner * strip_count + jitter, stable=True)
    return order.astype(jnp.int32).reshape(N_FRONT, NAB)


def draw_slot_tiles(key, part):
    return slot_layout(jax.random.fold_in(key, 11))


def draw_anc_tiles(key, part):
    slots = slot_layout(jax.random.fold_in(key, 11)).reshape(-1)
    order_all = NAB * BLK
    noise = jax.random.normal(jax.random.fold_in(key, 12), (order_all, order_all), jnp.float32)
    matrix = (noise + noise.T) * (0.3 / math.sqrt(2.0))
    diagonal = jax.random.uniform(jax.random.fold_in(key, 13), (order_all,), jnp.float32, 1.5, 3.0)
    matrix = matrix + jnp.diag(diagonal)
    matrix = jnp.clip(matrix, -50.0, 50.0)
    strips = matrix.reshape(NAB, STRIPS, SR, NAB, BLK).transpose(0, 3, 1, 2, 4).reshape(NAB * NAB * STRIPS, SR, BLK)
    return strips[slots].reshape(-1, BLK).astype(jnp.bfloat16)


def draw_sep_factor(key, part):
    total_rows = N_FRONT * NS
    noise = jax.random.normal(jax.random.fold_in(key, 21), (total_rows, NS), jnp.float32) * (1.0 / math.sqrt(NS))
    noise = jnp.clip(noise, -1.0, 1.0)
    diagonal = jnp.exp(jax.random.uniform(jax.random.fold_in(key, 22), (total_rows,), jnp.float32, 0.0, math.log(3.0)))
    ratio = jax.random.uniform(jax.random.fold_in(key, 23), (total_rows,), jnp.float32, 0.4, 0.85)
    local_row = jnp.arange(total_rows) % NS
    column = jnp.arange(NS)
    below = local_row[:, None] > column[None, :]
    on_diag = local_row[:, None] == column[None, :]
    next_to = local_row[:, None] == column[None, :] + 1
    result = jnp.where(below & ~next_to, noise, 0.0)
    result = result + jnp.where(on_diag, diagonal[:, None], 0.0)
    result = result + jnp.where(next_to, -(ratio * diagonal)[:, None], 0.0)
    return result.astype(jnp.bfloat16)


def draw_coup_list(key, part):
    keys = jax.random.split(jax.random.fold_in(key, 31), N_FRONT)
    perms = jax.vmap(lambda front_key: jax.random.permutation(front_key, NAB))(keys)[:, :MAXB]
    counts = jax.random.randint(jax.random.fold_in(key, 32), (N_FRONT,), MAXB // 4, MAXB + 1)
    heavy = jax.random.randint(jax.random.fold_in(key, 33), (), 0, N_FRONT)
    counts = jnp.where(jnp.arange(N_FRONT) == heavy, MAXB, counts)
    position = jnp.arange(MAXB)
    return jnp.where(position[None, :] < counts[:, None], perms, -1).astype(jnp.int32)


def level_of(own_key, extent, cuts, low, largest):
    factor_of = 1.0
    for dim, parts in cuts:
        heights = jax.random.uniform(jax.random.fold_in(jax.random.fold_in(own_key, 6), dim), (parts,), jnp.float32, low / len(cuts), largest / len(cuts))
        factor_of = factor_of * jnp.repeat(jnp.exp(heights), extent[dim] // parts).reshape((-1,) + (1,) * (len(extent) - 1 - dim))
    return factor_of


def normal_values(stream_key, dims, spread, reach, shards=(), held_as=jnp.bfloat16):
    values = jax.random.normal(stream_key, dims, jnp.float32) * spread
    if len(shards) > 0:
        values = level_of(stream_key, dims, shards, -0.22, 0.18) * values
    return jnp.clip(values, min=-reach, max=reach).astype(held_as)


def setup_inputs(seed: int = 0) -> dict:
    key_of = jax.random.split(jax.random.key(seed), 6)
    return {
        "sep_factor": draw_sep_factor(jax.random.fold_in(key_of[5], 71), 0),
        "coup_factor": normal_values(key_of[1], (N_FRONT * MAXA, NS), NS ** -0.5, 0.1875, ((0, 128),)),
        "coup_list": draw_coup_list(jax.random.fold_in(key_of[5], 71), 0),
        "slot_tiles": draw_slot_tiles(jax.random.fold_in(key_of[5], 71), 0),
        "anc_tiles": draw_anc_tiles(jax.random.fold_in(key_of[5], 71), 0),
    }


def reference(sep_factor, coup_factor, coup_list, slot_tiles, anc_tiles):
    pool_strips = jnp.zeros((NAB * NAB * STRIPS, SR, BLK), anc_tiles.dtype)
    pool_strips = pool_strips.at[slot_tiles.reshape(-1)].set(anc_tiles.reshape(-1, SR, BLK))
    pool_tiles = pool_strips.reshape(NAB, NAB, BLK, BLK)
    identity = jnp.eye(NS, dtype=jnp.float32)

    def per_front(front_index):
        lower_full = lax.dynamic_slice_in_dim(sep_factor, front_index * NS, NS, 0).astype(jnp.float32)
        inverse = lax.linalg.triangular_solve(lower_full, identity, left_side=True, lower=True)
        coupling = lax.dynamic_slice_in_dim(coup_factor, front_index * MAXA, MAXA, 0)
        blocks = coup_list[front_index]
        live_blocks = blocks >= 0
        safe_blocks = jnp.where(live_blocks, blocks, 0)
        row_live = jnp.repeat(live_blocks, BLK)
        coupling = jnp.where(row_live[:, None], coupling, jnp.zeros_like(coupling))
        wide_full = jnp.dot(coupling.astype(jnp.float32), inverse.astype(jnp.bfloat16).astype(jnp.float32), preferred_element_type=jnp.float32).astype(jnp.bfloat16)
        picked = pool_tiles[safe_blocks][:, safe_blocks]
        both_live = live_blocks[:, None] & live_blocks[None, :]
        picked = jnp.where(both_live[:, :, None, None], picked, jnp.zeros_like(picked))
        sigma_pair = picked.transpose(0, 2, 1, 3).reshape(MAXA, MAXA)
        carried = jnp.dot(sigma_pair.astype(jnp.float32), wide_full.astype(jnp.float32), preferred_element_type=jnp.float32).astype(jnp.bfloat16)
        product = jnp.dot(wide_full.T.astype(jnp.float32), carried.astype(jnp.float32), preferred_element_type=jnp.float32)
        inverse_square = jnp.dot(inverse.T, inverse, precision=lax.Precision.HIGHEST)
        selected = inverse_square + product
        return (selected, jnp.diagonal(selected))
    selected_all, variances = lax.map(per_front, jnp.arange(N_FRONT, dtype=jnp.int32))
    return (selected_all.reshape(N_FRONT * NS, NS), variances.reshape(N_FRONT * NS))
```

```python
import jax
import jax.numpy as jnp
import numpy as np
from jax import lax
from jax.experimental import pallas as pl
from jax.experimental.pallas import tpu as pltpu
from jax.sharding import PartitionSpec as P

AXES = ("front", "panel")
BLOCK = 128
STRIP = 32
NABOVE = 16
HALF = NABOVE // 2
SIDE = 1024
ROWS = SIDE // 2
F32 = jnp.float32
BF16 = jnp.bfloat16
VMEM = pl.BlockSpec(memory_space=pltpu.VMEM)
SMEM = pl.BlockSpec(memory_space=pltpu.SMEM)
LIMIT = 56 * 1024 * 1024


def params():
    return pltpu.CompilerParams(vmem_limit_bytes=LIMIT)


def cost(macs, moved):
    return pl.CostEstimate(flops=2 * macs, bytes_accessed=moved, transcendentals=0)


def dot(a, b):
    return jnp.dot(a, b, preferred_element_type=F32)


def dot_tn(a, b):
    return lax.dot_general(a, b, (((0,), (0,)), ((), ())), preferred_element_type=F32)


def split(x):
    hi = x.astype(BF16)
    return hi, (x - hi.astype(F32)).astype(BF16)


def spread(bits, step):
    return step * ((((bits >> 2) & 1) << 4) | (((bits >> 1) & 1) << 2) | (bits & 1))


def steps_of(core):
    return ((1, 3), (3, 1))[core]


def lowest(group, step):
    if step == 1:
        return group & 0b101010
    return group ^ (3 * ((group >> 1) & 0b010101))


def cubes(phase):
    out = []
    for core in range(2):
        step = steps_of(core)[phase]
        for first in range(64):
            if lowest(first, step) == first:
                out.append([(first ^ spread(bits, step)) * 2 + core for bits in range(8)])
    return out


def gather_cube(parts, phase):
    return lax.all_to_all(
        parts, AXES, split_axis=0, concat_axis=0, tiled=True, axis_index_groups=cubes(phase)
    )


def pick_kernel(where_ref, slots_ref, strips_ref, out_ref):
    core, group = where_ref[0], where_ref[1]
    for slot in range(NABOVE):
        row = slots_ref[group * NABOVE + slot] // 64 - core * HALF

        @pl.when((row >= 0) & (row < HALF))
        def _():
            strip = strips_ref[slot * STRIP : (slot + 1) * STRIP, :]
            for copy in range(8):
                at = pl.multiple_of(copy * HALF * STRIP + row * STRIP, STRIP)
                out_ref[pl.ds(at, STRIP), :] = strip


def pick_strips(where, slots, strips):
    return pl.pallas_call(
        pick_kernel,
        out_shape=jax.ShapeDtypeStruct((8 * HALF * STRIP, BLOCK), BF16),
        in_specs=[SMEM, SMEM, VMEM],
        out_specs=VMEM,
        compiler_params=params(),
        cost_estimate=cost(0, 1 << 20),
        name="pick_strips",
    )(where, slots, strips)


def invert_kernel(where_ref, mine_ref, other_ref, hi_ref, lo_ref, low_ref):
    core = where_ref[0]
    low_ref[pl.ds(pl.multiple_of(core * ROWS, ROWS), ROWS), :] = mine_ref[...]
    low_ref[pl.ds(pl.multiple_of((1 - core) * ROWS, ROWS), ROWS), :] = other_ref[...]
    hi_ref[...] = jnp.zeros_like(hi_ref)
    lo_ref[...] = jnp.zeros_like(lo_ref)
    row = lax.broadcasted_iota(jnp.int32, (BLOCK, BLOCK), 0)
    col = lax.broadcasted_iota(jnp.int32, (BLOCK, BLOCK), 1)
    differ = row ^ col
    below = row > col
    factors, inverses = [], []
    for b in range(8):
        at = slice(b * BLOCK, (b + 1) * BLOCK)
        factor = low_ref[at, at].astype(F32)
        diag = jnp.where(row == col, factor, 0.0)
        by_row = 1.0 / jnp.sum(diag, axis=1, keepdims=True)
        by_col = 1.0 / jnp.sum(diag, axis=0, keepdims=True)
        next_to = jnp.where(below & (differ < 2), factor, 0.0)
        inverses.append(jnp.where(row == col, by_row, 0.0) - by_row * next_to * by_col)
        factors.append(factor)
    size = 2
    while size < BLOCK:
        mask = below & (differ >= size) & (differ < 2 * size)
        for b in range(8):
            hi, lo = split(inverses[b])
            corner = jnp.where(mask, factors[b], 0.0).astype(BF16)
            both = dot(corner, jnp.concatenate([hi, lo], axis=1))
            t_hi, t_lo = split(both[:, :BLOCK] + both[:, BLOCK:])
            stacked = jnp.concatenate(
                [
                    jnp.concatenate([t_hi, t_lo], axis=1),
                    jnp.concatenate([t_hi, jnp.zeros_like(t_hi)], axis=1),
                ],
                axis=0,
            )
            both = dot(jnp.concatenate([hi, lo], axis=1), stacked)
            inverses[b] = inverses[b] - (both[:, :BLOCK] + both[:, BLOCK:])
        size *= 2
    for b in range(8):
        at = slice(b * BLOCK, (b + 1) * BLOCK)
        hi_ref[at, at], lo_ref[at, at] = split(inverses[b])
    while size < SIDE:
        for start in range(0, SIDE, 2 * size):
            first, second = slice(start, start + size), slice(start + size, start + 2 * size)
            corner = low_ref[second, first]
            t_hi, t_lo = split(dot(corner, hi_ref[first, first]) + dot(corner, lo_ref[first, first]))
            hi, lo = hi_ref[second, second], lo_ref[second, second]
            hi_ref[second, first], lo_ref[second, first] = split(
                -(dot(hi, t_hi) + dot(hi, t_lo) + dot(lo, t_hi))
            )
        size *= 2


def invert(where, mine, other):
    full = jax.ShapeDtypeStruct((SIDE, SIDE), BF16)
    return pl.pallas_call(
        invert_kernel,
        out_shape=(full, full),
        in_specs=[SMEM, VMEM, VMEM],
        out_specs=(VMEM, VMEM),
        scratch_shapes=[pltpu.VMEM((SIDE, SIDE), BF16)],
        compiler_params=params(),
        cost_estimate=cost(5 << 30, 6 << 20),
        name="invert",
    )(where, mine, other)


def wide_kernel(coupling_ref, hi_ref, out_ref):
    tile = 256
    for n in range(0, SIDE, tile):
        out_ref[:, n : n + tile] = dot(coupling_ref[:, n:], hi_ref[n:, n : n + tile]).astype(BF16)


def make_wide(coupling, hi):
    return pl.pallas_call(
        wide_kernel,
        out_shape=jax.ShapeDtypeStruct((SIDE, SIDE), BF16),
        in_specs=[VMEM, VMEM],
        out_specs=VMEM,
        compiler_params=params(),
        cost_estimate=cost(1 << 30, 6 << 20),
        name="make_wide",
    )(coupling, hi)


def square_kernel(where_ref, hi_ref, lo_ref, out_ref):
    mine = pl.ds(pl.multiple_of(where_ref[0] * ROWS, ROWS), ROWS)
    tile = 256
    for n in range(0, SIDE, tile):
        columns = slice(n, n + tile)
        hi, lo = hi_ref[n:, columns], lo_ref[n:, columns]
        left = hi_ref[n:, mine]
        out_ref[:, columns] = dot_tn(left, hi) + dot_tn(left, lo) + dot_tn(lo_ref[n:, mine], hi)


def make_square(where, hi, lo):
    return pl.pallas_call(
        square_kernel,
        out_shape=jax.ShapeDtypeStruct((ROWS, SIDE), F32),
        in_specs=[SMEM, VMEM, VMEM],
        out_specs=VMEM,
        compiler_params=params(),
        cost_estimate=cost(1 << 30, 6 << 20),
        name="make_square",
    )(where, hi, lo)


def place_kernel(where_ref, list_ref, mine_ref, other_ref, out_ref):
    core, group = where_ref[0], where_ref[1]
    out_ref[...] = jnp.zeros_like(out_ref)
    for a in range(NABOVE):
        owner, at = a // HALF, (a % HALF) * BLOCK
        block = list_ref[group * NABOVE + a]
        rows = pl.ds(pl.multiple_of(jnp.maximum(block, 0) * BLOCK, BLOCK), BLOCK)

        @pl.when((block >= 0) & (core == owner))
        def _():
            out_ref[rows, :] = mine_ref[at : at + BLOCK, :]

        @pl.when((block >= 0) & (core != owner))
        def _():
            out_ref[rows, :] = other_ref[at : at + BLOCK, :]


def place_wide(where, lists, mine, other):
    return pl.pallas_call(
        place_kernel,
        out_shape=jax.ShapeDtypeStruct((NABOVE * BLOCK, SIDE), BF16),
        in_specs=[SMEM, SMEM, VMEM, VMEM],
        out_specs=VMEM,
        compiler_params=params(),
        cost_estimate=cost(0, 8 << 20),
        name="place_wide",
    )(where, lists, mine, other)


def carry_kernel(where_ref, places_ref, strips_ref, wide_ref, carried_ref, send_ref, sigma_ref):
    core, group = where_ref[0], where_ref[1]
    first, second = jnp.where(core == 0, 1, 3), jnp.where(core == 0, 3, 1)

    def base(g, step):
        return jnp.where(step == 1, g & 0b101010, g ^ (3 * ((g >> 1) & 0b010101)))

    @pl.loop(0, 64)
    def _(n):
        middle = base(group, second) ^ spread(n >> 3, second)
        source = base(middle, first) ^ spread(n & 7, first)
        for row in range(HALF):
            place = places_ref[source * HALF + row]
            to = pl.multiple_of(row * BLOCK + (place & 3) * STRIP, STRIP)
            across = pl.multiple_of((place >> 2) * BLOCK, BLOCK)
            at = pl.multiple_of(n * HALF * STRIP + row * STRIP, STRIP)
            sigma_ref[pl.ds(to, STRIP), pl.ds(across, BLOCK)] = strips_ref[pl.ds(at, STRIP), :]

    tile = 256
    for n in range(0, SIDE, tile):
        carried_ref[:, n : n + tile] = dot(sigma_ref[...], wide_ref[:, n : n + tile]).astype(BF16)
    mine = pl.ds(pl.multiple_of(core * SIDE, SIDE), SIDE)
    theirs = pl.ds(pl.multiple_of((1 - core) * ROWS, ROWS), ROWS)
    for n in range(0, SIDE, tile):
        send_ref[:, n : n + tile] = dot_tn(wide_ref[mine, theirs], carried_ref[:, n : n + tile]).astype(BF16)


def carry(where, places, strips, wide):
    return pl.pallas_call(
        carry_kernel,
        out_shape=(
            jax.ShapeDtypeStruct((SIDE, SIDE), BF16),
            jax.ShapeDtypeStruct((ROWS, SIDE), BF16),
        ),
        in_specs=[SMEM, SMEM, VMEM, VMEM],
        out_specs=(VMEM, VMEM),
        scratch_shapes=[pltpu.VMEM((SIDE, NABOVE * BLOCK), BF16)],
        compiler_params=params(),
        cost_estimate=cost(5 << 29, 12 << 20),
        name="carry",
    )(where, places, strips, wide)


def own_kernel(where_ref, wide_ref, carried_ref, square_ref, out_ref):
    core = where_ref[0]
    rows = pl.ds(pl.multiple_of(core * SIDE, SIDE), SIDE)
    mine = pl.ds(pl.multiple_of(core * ROWS, ROWS), ROWS)
    tile = 256
    for n in range(0, SIDE, tile):
        columns = slice(n, n + tile)
        out_ref[:, columns] = square_ref[:, columns] + dot_tn(wide_ref[rows, mine], carried_ref[:, columns])


def own_product(where, wide, carried, square):
    return pl.pallas_call(
        own_kernel,
        out_shape=jax.ShapeDtypeStruct((ROWS, SIDE), F32),
        in_specs=[SMEM, VMEM, VMEM, VMEM],
        out_specs=VMEM,
        compiler_params=params(),
        cost_estimate=cost(1 << 29, 8 << 20),
        name="own_product",
    )(where, wide, carried, square)


def finish_kernel(where_ref, own_ref, received_ref, out_ref, diag_ref):
    out_ref[...] = own_ref[...] + received_ref[...].astype(F32)
    block = out_ref[:, pl.ds(pl.multiple_of(where_ref[0] * ROWS, ROWS), ROWS)]
    row = lax.broadcasted_iota(jnp.int32, (ROWS, ROWS), 0)
    col = lax.broadcasted_iota(jnp.int32, (ROWS, ROWS), 1)
    diag_ref[...] = jnp.sum(jnp.where(row == col, block, 0.0), axis=0, keepdims=True)


def finish(where, own, received):
    return pl.pallas_call(
        finish_kernel,
        out_shape=(
            jax.ShapeDtypeStruct((ROWS, SIDE), F32),
            jax.ShapeDtypeStruct((1, ROWS), F32),
        ),
        in_specs=[SMEM, VMEM, VMEM],
        out_specs=(VMEM, VMEM),
        compiler_params=params(),
        cost_estimate=cost(0, 6 << 20),
        name="finish",
    )(where, own, received)


def swap(x):
    return lax.ppermute(x, "panel", [(0, 1), (1, 0)])


def on_device(sep_factor, coup_factor, coup_list, slot_tiles, anc_tiles):
    core = lax.axis_index("panel")
    group = lax.axis_index("front")
    where = jnp.stack([core, group]).astype(jnp.int32)
    lists = coup_list.reshape(-1)
    slots = slot_tiles.reshape(-1)
    wanted = core * HALF + jnp.arange(HALF, dtype=jnp.int32)
    hit = (slot_tiles // 64)[:, None, :] == wanted[None, :, None]
    places = jnp.sum(jnp.where(hit, (slot_tiles % 64)[:, None, :], 0), axis=2).reshape(-1)

    sep_other = swap(sep_factor)
    picked = pick_strips(where, slots, anc_tiles)
    near = gather_cube(picked, 0)
    strips = gather_cube(jnp.broadcast_to(near[None], (8,) + near.shape).reshape(-1, BLOCK), 1)

    hi, lo = invert(where, sep_factor, sep_other)
    wide_mine = make_wide(coup_factor, hi)
    wide_other = swap(wide_mine)
    square = make_square(where, hi, lo)
    wide = place_wide(where, lists, wide_mine, wide_other)
    carried, to_send = carry(where, places, strips, wide)
    received = swap(to_send)
    own = own_product(where, wide, carried, square)
    selected, variances = finish(where, own, received)
    return selected, variances.reshape(ROWS)


def solution(mesh):
    placed = (P(AXES, None), P(AXES, None), P(), P(), P("front", None))
    return jax.shard_map(
        on_device,
        mesh=mesh,
        in_specs=placed,
        out_specs=(P(AXES, None), P(AXES)),
        check_vma=False,
    )
```

```python
import jax
import jax.numpy as jnp
import numpy as np
from jax import lax
from jax.experimental import pallas as pl
from jax.experimental.pallas import tpu as pltpu
from jax.sharding import PartitionSpec as P

AXES = ("front", "panel")
BLOCK = 128
STRIP = 32
NABOVE = 16
HALF = NABOVE // 2
SIDE = 1024
ROWS = SIDE // 2
F32 = jnp.float32
BF16 = jnp.bfloat16
VMEM = pl.BlockSpec(memory_space=pltpu.VMEM)
SMEM = pl.BlockSpec(memory_space=pltpu.SMEM)
MIB = 1024 * 1024


def params(mib):
    return pltpu.CompilerParams(vmem_limit_bytes=mib * MIB)


def cost(macs, moved):
    return pl.CostEstimate(flops=2 * macs, bytes_accessed=moved, transcendentals=0)


def dot(a, b):
    return jnp.dot(a, b, preferred_element_type=F32)


def dot_tn(a, b):
    return lax.dot_general(a, b, (((0,), (0,)), ((), ())), preferred_element_type=F32)


def split(x):
    hi = x.astype(BF16)
    return hi, (x - hi.astype(F32)).astype(BF16)


def spread(bits, step):
    return step * ((((bits >> 2) & 1) << 4) | (((bits >> 1) & 1) << 2) | (bits & 1))


def steps_of(core):
    return ((1, 3), (3, 1))[core]


def lowest(group, step):
    if step == 1:
        return group & 0b101010
    return group ^ (3 * ((group >> 1) & 0b010101))


def cubes(phase):
    out = []
    for core in range(2):
        step = steps_of(core)[phase]
        for first in range(64):
            if lowest(first, step) == first:
                out.append([(first ^ spread(bits, step)) * 2 + core for bits in range(8)])
    return out


def gather_cube(parts, phase):
    return lax.all_to_all(
        parts, AXES, split_axis=0, concat_axis=0, tiled=True, axis_index_groups=cubes(phase)
    )


def pick_kernel(slots_ref, table_ref, strips_ref, out_ref, places_ref):
    core, group = lax.axis_index("panel"), lax.axis_index("front")
    for slot in range(NABOVE):
        row = slots_ref[slot, group] // 64 - core * HALF

        @pl.when((row >= 0) & (row < HALF))
        def _():
            strip = strips_ref[slot * STRIP : (slot + 1) * STRIP, :]
            for copy in range(8):
                at = pl.multiple_of(copy * HALF * STRIP + row * STRIP, STRIP)
                out_ref[pl.ds(at, STRIP), :] = strip

    ids = table_ref[...]
    for row in range(HALF):
        hit = (ids >> 6) == core * HALF + row
        places_ref[row : row + 1, :] = jnp.sum(jnp.where(hit, ids & 63, 0), axis=0, keepdims=True)


def pick_strips(slots, strips):
    return pl.pallas_call(
        pick_kernel,
        out_shape=(
            jax.ShapeDtypeStruct((8 * HALF * STRIP, BLOCK), BF16),
            jax.ShapeDtypeStruct((HALF, 64), jnp.int32),
        ),
        in_specs=[SMEM, VMEM, VMEM],
        out_specs=(VMEM, VMEM),
        compiler_params=params(4),
        cost_estimate=cost(0, 1 << 20),
        name="pick_strips",
    )(slots, slots, strips)


def solve_kernel(mine_ref, other_ref, coupling_ref, wide_ref, square_ref, low_ref, hi_ref, lo_ref):
    core = lax.axis_index("panel")
    low_ref[pl.ds(pl.multiple_of(core * ROWS, ROWS), ROWS), :] = mine_ref[...]
    low_ref[pl.ds(pl.multiple_of((1 - core) * ROWS, ROWS), ROWS), :] = other_ref[...]
    hi_ref[...] = jnp.zeros_like(hi_ref)
    lo_ref[...] = jnp.zeros_like(lo_ref)
    row = lax.broadcasted_iota(jnp.int32, (BLOCK, BLOCK), 0)
    col = lax.broadcasted_iota(jnp.int32, (BLOCK, BLOCK), 1)
    differ = row ^ col
    below = row > col
    factors, inverses = [], []
    for b in range(8):
        at = slice(b * BLOCK, (b + 1) * BLOCK)
        factor = low_ref[at, at].astype(F32)
        diag = jnp.where(row == col, factor, 0.0)
        by_row = 1.0 / jnp.sum(diag, axis=1, keepdims=True)
        by_col = 1.0 / jnp.sum(diag, axis=0, keepdims=True)
        next_to = jnp.where(below & (differ < 2), factor, 0.0)
        inverses.append(jnp.where(row == col, by_row, 0.0) - by_row * next_to * by_col)
        factors.append(factor)
    size = 2
    while size < BLOCK:
        mask = below & (differ >= size) & (differ < 2 * size)
        for b in range(8):
            hi, lo = split(inverses[b])
            corner = jnp.where(mask, factors[b], 0.0).astype(BF16)
            both = dot(corner, jnp.concatenate([hi, lo], axis=1))
            t_hi, t_lo = split(both[:, :BLOCK] + both[:, BLOCK:])
            stacked = jnp.concatenate(
                [
                    jnp.concatenate([t_hi, t_lo], axis=1),
                    jnp.concatenate([t_hi, jnp.zeros_like(t_hi)], axis=1),
                ],
                axis=0,
            )
            both = dot(jnp.concatenate([hi, lo], axis=1), stacked)
            inverses[b] = inverses[b] - (both[:, :BLOCK] + both[:, BLOCK:])
        size *= 2
    for b in range(8):
        at = slice(b * BLOCK, (b + 1) * BLOCK)
        hi_ref[at, at], lo_ref[at, at] = split(inverses[b])
    while size < SIDE:
        for start in range(0, SIDE, 2 * size):
            first, second = slice(start, start + size), slice(start + size, start + 2 * size)
            corner = low_ref[second, first]
            t_hi, t_lo = split(dot(corner, hi_ref[first, first]) + dot(corner, lo_ref[first, first]))
            hi, lo = hi_ref[second, second], lo_ref[second, second]
            hi_ref[second, first], lo_ref[second, first] = split(
                -(dot(hi, t_hi) + dot(hi, t_lo) + dot(lo, t_hi))
            )
        size *= 2
    tile = 256
    for n in range(0, SIDE, tile):
        columns = slice(n, n + tile)
        wide_ref[:, columns] = dot(coupling_ref[:, n:], hi_ref[n:, columns]).astype(BF16)
    mine = pl.ds(pl.multiple_of(core * ROWS, ROWS), ROWS)
    for n in range(0, SIDE, tile):
        columns = slice(n, n + tile)
        hi, lo = hi_ref[n:, columns], lo_ref[n:, columns]
        left = hi_ref[n:, mine]
        square_ref[:, columns] = dot_tn(left, hi) + dot_tn(left, lo) + dot_tn(lo_ref[n:, mine], hi)


def solve(mine, other, coupling):
    return pl.pallas_call(
        solve_kernel,
        out_shape=(
            jax.ShapeDtypeStruct((SIDE, SIDE), BF16),
            jax.ShapeDtypeStruct((ROWS, SIDE), F32),
        ),
        in_specs=[VMEM, VMEM, VMEM],
        out_specs=(VMEM, VMEM),
        scratch_shapes=[pltpu.VMEM((SIDE, SIDE), BF16)] * 3,
        compiler_params=params(20),
        cost_estimate=cost(4 << 30, 8 << 20),
        name="solve",
    )(mine, other, coupling)


def turn_kernel(list_ref, mine_ref, other_ref, out_ref):
    core, group = lax.axis_index("panel"), lax.axis_index("front")
    out_ref[...] = jnp.zeros_like(out_ref)
    for a in range(NABOVE):
        owner, at = a // HALF, (a % HALF) * BLOCK
        row = list_ref[a, group] - core * HALF
        columns = pl.ds(pl.multiple_of(jnp.clip(row, 0, HALF - 1) * BLOCK, BLOCK), BLOCK)
        wanted = (row >= 0) & (row < HALF) & (list_ref[a, group] >= 0)

        @pl.when(wanted & (core == owner))
        def _():
            out_ref[:, columns] = mine_ref[at : at + BLOCK, :].astype(F32).T.astype(BF16)

        @pl.when(wanted & (core != owner))
        def _():
            out_ref[:, columns] = other_ref[at : at + BLOCK, :].astype(F32).T.astype(BF16)


def turn_wide(lists, mine, other):
    return pl.pallas_call(
        turn_kernel,
        out_shape=jax.ShapeDtypeStruct((SIDE, SIDE), BF16),
        in_specs=[SMEM, VMEM, VMEM],
        out_specs=VMEM,
        compiler_params=params(12),
        cost_estimate=cost(0, 8 << 20),
        name="turn_wide",
    )(lists, mine, other)


def carry_kernel(
    list_ref, places_ref, strips_ref, mine_ref, other_ref, turned_ref, carried_ref, send_ref, sigma_ref, column_ref
):
    core, group = lax.axis_index("panel"), lax.axis_index("front")
    first, second = jnp.where(core == 0, 1, 3), jnp.where(core == 0, 3, 1)

    def base(g, step):
        return jnp.where(step == 1, g & 0b101010, g ^ (3 * ((g >> 1) & 0b010101)))

    for block in range(NABOVE):
        column_ref[block] = NABOVE * BLOCK
    for a in range(NABOVE):
        block = list_ref[a, group]
        column = pl.multiple_of((a ^ (core * HALF)) * BLOCK, BLOCK)

        @pl.when(block >= 0)
        def _():
            column_ref[block] = column

        @pl.when(block < 0)
        def _():
            sigma_ref[:, pl.ds(column, BLOCK)] = jnp.zeros((SIDE, BLOCK), BF16)

    @pl.loop(0, 64)
    def _(n):
        middle = base(group, second) ^ spread(n >> 3, second)
        source = base(middle, first) ^ spread(n & 7, first)
        for row in range(HALF):
            place = places_ref[row, source]
            to = pl.multiple_of(row * BLOCK + (place & 3) * STRIP, STRIP)
            across = pl.multiple_of(column_ref[place >> 2], BLOCK)
            at = pl.multiple_of(n * HALF * STRIP + row * STRIP, STRIP)
            sigma_ref[pl.ds(to, STRIP), pl.ds(across, BLOCK)] = strips_ref[pl.ds(at, STRIP), :]

    tile = 256
    for n in range(0, SIDE, tile):
        columns = slice(n, n + tile)
        carried_ref[:, columns] = (
            dot(sigma_ref[:, :SIDE], mine_ref[:, columns])
            + dot(sigma_ref[:, SIDE : 2 * SIDE], other_ref[:, columns])
        ).astype(BF16)
    theirs = pl.ds(pl.multiple_of((1 - core) * ROWS, ROWS), ROWS)
    for n in range(0, SIDE, tile):
        columns = slice(n, n + tile)
        send_ref[:, columns] = dot(turned_ref[theirs, :], carried_ref[:, columns]).astype(BF16)


def carry(lists, places, strips, mine, other, turned):
    return pl.pallas_call(
        carry_kernel,
        out_shape=(
            jax.ShapeDtypeStruct((SIDE, SIDE), BF16),
            jax.ShapeDtypeStruct((ROWS, SIDE), BF16),
        ),
        in_specs=[SMEM, SMEM, VMEM, VMEM, VMEM, VMEM],
        out_specs=(VMEM, VMEM),
        scratch_shapes=[
            pltpu.VMEM((SIDE, (NABOVE + 1) * BLOCK), BF16),
            pltpu.SMEM((NABOVE,), jnp.int32),
        ],
        compiler_params=params(24),
        cost_estimate=cost(5 << 29, 12 << 20),
        name="carry",
    )(lists, places, strips, mine, other, turned)


def own_kernel(turned_ref, carried_ref, square_ref, out_ref):
    mine = pl.ds(pl.multiple_of(lax.axis_index("panel") * ROWS, ROWS), ROWS)
    tile = 256
    for n in range(0, SIDE, tile):
        columns = slice(n, n + tile)
        out_ref[:, columns] = square_ref[:, columns] + dot(turned_ref[mine, :], carried_ref[:, columns])


def own_product(turned, carried, square):
    return pl.pallas_call(
        own_kernel,
        out_shape=jax.ShapeDtypeStruct((ROWS, SIDE), F32),
        in_specs=[VMEM, VMEM, VMEM],
        out_specs=VMEM,
        compiler_params=params(12),
        cost_estimate=cost(1 << 29, 8 << 20),
        name="own_product",
    )(turned, carried, square)


def finish_kernel(own_ref, received_ref, out_ref, diag_ref):
    out_ref[...] = own_ref[...] + received_ref[...].astype(F32)
    at = lax.axis_index("panel") * ROWS + pl.program_id(0) * BLOCK
    block = out_ref[:, pl.ds(pl.multiple_of(at, BLOCK), BLOCK)]
    row = lax.broadcasted_iota(jnp.int32, (BLOCK, BLOCK), 0)
    col = lax.broadcasted_iota(jnp.int32, (BLOCK, BLOCK), 1)
    diag_ref[...] = jnp.sum(jnp.where(row == col, block, 0.0), axis=0, keepdims=True)


def finish(own, received):
    rows = pl.BlockSpec((BLOCK, SIDE), lambda t: (t, 0))
    return pl.pallas_call(
        finish_kernel,
        grid=(ROWS // BLOCK,),
        out_shape=(
            jax.ShapeDtypeStruct((ROWS, SIDE), F32),
            jax.ShapeDtypeStruct((1, ROWS), F32),
        ),
        in_specs=[rows, rows],
        out_specs=(rows, pl.BlockSpec((1, BLOCK), lambda t: (0, t))),
        compiler_params=params(6),
        cost_estimate=cost(0, 6 << 20),
        name="finish",
    )(own, received)


def swap(x):
    return lax.ppermute(x, "panel", [(0, 1), (1, 0)])


def on_device(sep_factor, coup_factor, coup_list, slot_tiles, anc_tiles):
    lists, slots = coup_list.T, slot_tiles.T
    sep_other = swap(sep_factor)
    picked, places = pick_strips(slots, anc_tiles)
    near = gather_cube(picked, 0)
    strips = gather_cube(jnp.broadcast_to(near[None], (8,) + near.shape).reshape(-1, BLOCK), 1)
    wide_mine, square = solve(sep_factor, sep_other, coup_factor)
    wide_other = swap(wide_mine)
    turned = turn_wide(lists, wide_mine, wide_other)
    carried, to_send = carry(lists, places, strips, wide_mine, wide_other, turned)
    received = swap(to_send)
    own = own_product(turned, carried, square)
    selected, variances = finish(own, received)
    return selected, variances.reshape(ROWS)


def solution(mesh):
    placed = (P(AXES, None), P(AXES, None), P(), P(), P("front", None))
    return jax.shard_map(
        on_device,
        mesh=mesh,
        in_specs=placed,
        out_specs=(P(AXES, None), P(AXES)),
        check_vma=False,
    )
```

```python
import jax
import jax.numpy as jnp
import numpy as np
from jax import lax
from jax.experimental import pallas as pl
from jax.experimental.pallas import tpu as pltpu
from jax.sharding import PartitionSpec as P

AXES = ("front", "panel")
BLOCK = 128
STRIP = 32
NABOVE = 16
HALF = NABOVE // 2
SIDE = 1024
ROWS = SIDE // 2
F32 = jnp.float32
BF16 = jnp.bfloat16
VMEM = pl.BlockSpec(memory_space=pltpu.VMEM)
ANY = pl.BlockSpec(memory_space=pl.ANY)
SMEM = pl.BlockSpec(memory_space=pltpu.SMEM)
MIB = 1024 * 1024


def params(mib):
    return pltpu.CompilerParams(vmem_limit_bytes=mib * MIB)


def cost(macs, moved):
    return pl.CostEstimate(flops=2 * macs, bytes_accessed=moved, transcendentals=0)


def dot(a, b):
    return jnp.dot(a, b, preferred_element_type=F32)


def dot_tn(a, b):
    return lax.dot_general(a, b, (((0,), (0,)), ((), ())), preferred_element_type=F32)


def split(x):
    hi = x.astype(BF16)
    return hi, (x - hi.astype(F32)).astype(BF16)


def spread(bits, step):
    return step * ((((bits >> 2) & 1) << 4) | (((bits >> 1) & 1) << 2) | (bits & 1))


def steps_of(core):
    return ((1, 3), (3, 1))[core]


def lowest(group, step):
    if step == 1:
        return group & 0b101010
    return group ^ (3 * ((group >> 1) & 0b010101))


def cubes(phase):
    out = []
    for core in range(2):
        step = steps_of(core)[phase]
        for first in range(64):
            if lowest(first, step) == first:
                out.append([(first ^ spread(bits, step)) * 2 + core for bits in range(8)])
    return out


def gather_cube(parts, phase):
    return lax.all_to_all(
        parts, AXES, split_axis=0, concat_axis=0, tiled=True, axis_index_groups=cubes(phase)
    )


def across(x, bits):
    pairs = []
    for group in range(64):
        for core in range(2):
            step = steps_of(core)[1]
            pairs.append((group * 2 + core, (group ^ spread(bits, step)) * 2 + core))
    return lax.ppermute(x, AXES, pairs)


def pick_kernel(slots_ref, table_ref, strips_ref, out_ref, places_ref):
    core, group = lax.axis_index("panel"), lax.axis_index("front")
    for slot in range(NABOVE):
        row = slots_ref[slot, group] // 64 - core * HALF

        @pl.when((row >= 0) & (row < HALF))
        def _():
            strip = strips_ref[slot * STRIP : (slot + 1) * STRIP, :]
            for copy in range(8):
                at = pl.multiple_of(copy * HALF * STRIP + row * STRIP, STRIP)
                out_ref[pl.ds(at, STRIP), :] = strip

    ids = table_ref[...]
    for row in range(HALF):
        hit = (ids >> 6) == core * HALF + row
        places_ref[row : row + 1, :] = jnp.sum(jnp.where(hit, ids & 63, 0), axis=0, keepdims=True)


def pick_strips(slots, strips):
    return pl.pallas_call(
        pick_kernel,
        out_shape=(
            jax.ShapeDtypeStruct((8 * HALF * STRIP, BLOCK), BF16),
            jax.ShapeDtypeStruct((HALF, 64), jnp.int32),
        ),
        in_specs=[SMEM, VMEM, VMEM],
        out_specs=(VMEM, VMEM),
        compiler_params=params(4),
        cost_estimate=cost(0, 1 << 20),
        name="pick_strips",
    )(slots, slots, strips)


def invert_kernel(mine_ref, other_ref, after_ref, hi_ref, lo_ref, low_ref):
    core = lax.axis_index("panel")
    low_ref[pl.ds(pl.multiple_of(core * ROWS, ROWS), ROWS), :] = mine_ref[...]
    low_ref[pl.ds(pl.multiple_of((1 - core) * ROWS, ROWS), ROWS), :] = other_ref[...]
    hi_ref[...] = jnp.zeros_like(hi_ref)
    lo_ref[...] = jnp.zeros_like(lo_ref)
    row = lax.broadcasted_iota(jnp.int32, (BLOCK, BLOCK), 0)
    col = lax.broadcasted_iota(jnp.int32, (BLOCK, BLOCK), 1)
    differ = row ^ col
    below = row > col
    factors, inverses = [], []
    for b in range(8):
        at = slice(b * BLOCK, (b + 1) * BLOCK)
        factor = low_ref[at, at].astype(F32)
        diag = jnp.where(row == col, factor, 0.0)
        by_row = 1.0 / jnp.sum(diag, axis=1, keepdims=True)
        by_col = 1.0 / jnp.sum(diag, axis=0, keepdims=True)
        next_to = jnp.where(below & (differ < 2), factor, 0.0)
        inverses.append(jnp.where(row == col, by_row, 0.0) - by_row * next_to * by_col)
        factors.append(factor)
    size = 2
    while size < BLOCK:
        mask = below & (differ >= size) & (differ < 2 * size)
        for b in range(8):
            hi, lo = split(inverses[b])
            corner = jnp.where(mask, factors[b], 0.0).astype(BF16)
            both = dot(corner, jnp.concatenate([hi, lo], axis=1))
            t_hi, t_lo = split(both[:, :BLOCK] + both[:, BLOCK:])
            stacked = jnp.concatenate(
                [
                    jnp.concatenate([t_hi, t_lo], axis=1),
                    jnp.concatenate([t_hi, jnp.zeros_like(t_hi)], axis=1),
                ],
                axis=0,
            )
            both = dot(jnp.concatenate([hi, lo], axis=1), stacked)
            inverses[b] = inverses[b] - (both[:, :BLOCK] + both[:, BLOCK:])
        size *= 2
    for b in range(8):
        at = slice(b * BLOCK, (b + 1) * BLOCK)
        hi_ref[at, at], lo_ref[at, at] = split(inverses[b])
    while size < SIDE:
        for start in range(0, SIDE, 2 * size):
            first, second = slice(start, start + size), slice(start + size, start + 2 * size)
            corner = low_ref[second, first]
            t_hi, t_lo = split(dot(corner, hi_ref[first, first]) + dot(corner, lo_ref[first, first]))
            hi, lo = hi_ref[second, second], lo_ref[second, second]
            hi_ref[second, first], lo_ref[second, first] = split(
                -(dot(hi, t_hi) + dot(hi, t_lo) + dot(lo, t_hi))
            )
        size *= 2


def invert(mine, other, after):
    full = jax.ShapeDtypeStruct((SIDE, SIDE), BF16)
    return pl.pallas_call(
        invert_kernel,
        out_shape=(full, full),
        in_specs=[VMEM, VMEM, ANY],
        out_specs=(VMEM, VMEM),
        scratch_shapes=[pltpu.VMEM((SIDE, SIDE), BF16)],
        compiler_params=params(12),
        cost_estimate=cost(1 << 20, 1 << 16),
        name="invert",
    )(mine, other, after)


def wide_kernel(coupling_ref, hi_ref, x_ref, y_ref, z_ref, wide_ref):
    tile = 256
    for n in range(0, SIDE, tile):
        columns = slice(n, n + tile)
        wide_ref[:, columns] = dot(coupling_ref[:, n:], hi_ref[n:, columns]).astype(BF16)


def make_wide(coupling, hi, after):
    return pl.pallas_call(
        wide_kernel,
        out_shape=jax.ShapeDtypeStruct((SIDE, SIDE), BF16),
        in_specs=[VMEM, VMEM, ANY, ANY, ANY],
        out_specs=VMEM,
        compiler_params=params(10),
        cost_estimate=cost(1 << 20, 1 << 16),
        name="make_wide",
    )(coupling, hi, *after)


def square_kernel(hi_ref, lo_ref, x_ref, y_ref, z_ref, square_ref):
    mine = pl.ds(pl.multiple_of(lax.axis_index("panel") * ROWS, ROWS), ROWS)
    tile = 256
    for n in range(0, SIDE, tile):
        columns = slice(n, n + tile)
        hi, lo = hi_ref[n:, columns], lo_ref[n:, columns]
        left = hi_ref[n:, mine]
        square_ref[:, columns] = dot_tn(left, hi) + dot_tn(left, lo) + dot_tn(lo_ref[n:, mine], hi)


def make_square(hi, lo, after):
    return pl.pallas_call(
        square_kernel,
        out_shape=jax.ShapeDtypeStruct((ROWS, SIDE), F32),
        in_specs=[VMEM, VMEM, ANY, ANY, ANY],
        out_specs=VMEM,
        compiler_params=params(10),
        cost_estimate=cost(1 << 20, 1 << 16),
        name="make_square",
    )(hi, lo, *after)


def turn_kernel(list_ref, places_ref, mine_ref, other_ref, x_ref, y_ref, z_ref, square_ref, out_ref, table_ref):
    core, group = lax.axis_index("panel"), lax.axis_index("front")
    places = places_ref[...]
    column = jnp.full(places.shape, NABOVE, jnp.int32)
    for a in range(NABOVE):
        column = jnp.where((places >> 2) == list_ref[a, group], a ^ (core * HALF), column)
    row = lax.broadcasted_iota(jnp.int32, places.shape, 0)
    table_ref[...] = column * SIDE + row * BLOCK + (places & 3) * STRIP
    out_ref[...] = jnp.zeros_like(out_ref)
    for a in range(NABOVE):
        owner, at = a // HALF, (a % HALF) * BLOCK
        row = list_ref[a, group] - core * HALF
        columns = pl.ds(pl.multiple_of(jnp.clip(row, 0, HALF - 1) * BLOCK, BLOCK), BLOCK)
        wanted = (row >= 0) & (row < HALF) & (list_ref[a, group] >= 0)

        @pl.when(wanted & (core == owner))
        def _():
            out_ref[:, columns] = mine_ref[at : at + BLOCK, :].astype(F32).T.astype(BF16)

        @pl.when(wanted & (core != owner))
        def _():
            out_ref[:, columns] = other_ref[at : at + BLOCK, :].astype(F32).T.astype(BF16)


def turn_wide(lists, places, mine, other, after):
    return pl.pallas_call(
        turn_kernel,
        out_shape=(
            jax.ShapeDtypeStruct((SIDE, SIDE), BF16),
            jax.ShapeDtypeStruct((HALF, 64), jnp.int32),
        ),
        in_specs=[SMEM, VMEM, VMEM, VMEM, ANY, ANY, ANY, ANY],
        out_specs=(VMEM, VMEM),
        compiler_params=params(12),
        cost_estimate=cost(1 << 20, 1 << 16),
        name="turn_wide",
    )(lists, places, mine, other, *after)


def carry_kernel(list_ref, table_ref, *refs):
    strips_refs, refs = refs[:8], refs[8:]
    mine_ref, other_ref, turned_ref, carried_ref, send_ref, sigma_ref = refs
    core, group = lax.axis_index("panel"), lax.axis_index("front")
    first, second = jnp.where(core == 0, 1, 3), jnp.where(core == 0, 3, 1)
    for a in range(NABOVE):
        column = pl.multiple_of((a ^ (core * HALF)) * SIDE, SIDE)

        @pl.when(list_ref[a, group] < 0)
        def _():
            sigma_ref[pl.ds(column, SIDE), :] = jnp.zeros((SIDE, BLOCK), BF16)

    for bits in range(8):
        middle = group ^ spread(bits, second)
        start = jnp.where(first == 1, middle & 0b101010, middle ^ (3 * ((middle >> 1) & 0b010101)))

        @pl.loop(0, 8)
        def _(n):
            source = start ^ spread(n, first)
            for row in range(HALF):
                to = pl.multiple_of(table_ref[row, source], STRIP)
                at = pl.multiple_of(n * HALF * STRIP + row * STRIP, STRIP)
                sigma_ref[pl.ds(to, STRIP), :] = strips_refs[bits][pl.ds(at, STRIP), :]

    def sigma(at):
        blocks = [sigma_ref[c * SIDE : (c + 1) * SIDE, :] for c in range(at, at + HALF)]
        return jnp.concatenate(blocks, axis=1)

    tile = 256
    for n in range(0, SIDE, tile):
        columns = slice(n, n + tile)
        carried_ref[:, columns] = (
            dot(sigma(0), mine_ref[:, columns]) + dot(sigma(HALF), other_ref[:, columns])
        ).astype(BF16)
    theirs = pl.ds(pl.multiple_of((1 - core) * ROWS, ROWS), ROWS)
    for n in range(0, SIDE, tile):
        columns = slice(n, n + tile)
        send_ref[:, columns] = dot(turned_ref[theirs, :], carried_ref[:, columns]).astype(BF16)


def carry(lists, table, strips, mine, other, turned):
    return pl.pallas_call(
        carry_kernel,
        out_shape=(
            jax.ShapeDtypeStruct((SIDE, SIDE), BF16),
            jax.ShapeDtypeStruct((ROWS, SIDE), BF16),
        ),
        in_specs=[SMEM, SMEM] + [VMEM] * 11,
        out_specs=(VMEM, VMEM),
        scratch_shapes=[pltpu.VMEM(((NABOVE + 1) * SIDE, BLOCK), BF16)],
        compiler_params=params(24),
        cost_estimate=cost(5 << 29, 12 << 20),
        name="carry",
    )(lists, table, *strips, mine, other, turned)


def own_kernel(turned_ref, carried_ref, square_ref, out_ref):
    mine = pl.ds(pl.multiple_of(lax.axis_index("panel") * ROWS, ROWS), ROWS)
    tile = 256
    for n in range(0, SIDE, tile):
        columns = slice(n, n + tile)
        out_ref[:, columns] = square_ref[:, columns] + dot(turned_ref[mine, :], carried_ref[:, columns])


def own_product(turned, carried, square):
    return pl.pallas_call(
        own_kernel,
        out_shape=jax.ShapeDtypeStruct((ROWS, SIDE), F32),
        in_specs=[VMEM, VMEM, VMEM],
        out_specs=VMEM,
        compiler_params=params(12),
        cost_estimate=cost(1 << 29, 8 << 20),
        name="own_product",
    )(turned, carried, square)


def finish_kernel(own_ref, received_ref, out_ref, diag_ref):
    out_ref[...] = own_ref[...] + received_ref[...].astype(F32)
    at = lax.axis_index("panel") * ROWS + pl.program_id(0) * BLOCK
    block = out_ref[:, pl.ds(pl.multiple_of(at, BLOCK), BLOCK)]
    row = lax.broadcasted_iota(jnp.int32, (BLOCK, BLOCK), 0)
    col = lax.broadcasted_iota(jnp.int32, (BLOCK, BLOCK), 1)
    diag_ref[...] = jnp.sum(jnp.where(row == col, block, 0.0), axis=0, keepdims=True)


def finish(own, received):
    rows = pl.BlockSpec((BLOCK, SIDE), lambda t: (t, 0))
    return pl.pallas_call(
        finish_kernel,
        grid=(ROWS // BLOCK,),
        out_shape=(
            jax.ShapeDtypeStruct((ROWS, SIDE), F32),
            jax.ShapeDtypeStruct((1, ROWS), F32),
        ),
        in_specs=[rows, rows],
        out_specs=(rows, pl.BlockSpec((1, BLOCK), lambda t: (0, t))),
        compiler_params=params(6),
        cost_estimate=cost(0, 6 << 20),
        name="finish",
    )(own, received)


def swap(x):
    return lax.ppermute(x, "panel", [(0, 1), (1, 0)])


def on_device(sep_factor, coup_factor, coup_list, slot_tiles, anc_tiles):
    lists, slots = coup_list.T, slot_tiles.T
    sep_other = swap(sep_factor)
    picked, places = pick_strips(slots, anc_tiles)
    near = gather_cube(picked, 0)
    hi, lo = invert(sep_factor, sep_other, near)
    x, y, z = across(near, 1), across(near, 2), across(near, 4)
    wide_mine = make_wide(coup_factor, hi, (x, y, z))
    wide_other = swap(wide_mine)
    xy, yz, zx = across(x, 2), across(y, 4), across(z, 1)
    square = make_square(hi, lo, (x, y, z))
    strips = [near, x, y, xy, z, zx, yz, across(xy, 4)]
    turned, table = turn_wide(lists, places, wide_mine, wide_other, (xy, yz, zx, square))
    carried, to_send = carry(lists, table, strips, wide_mine, wide_other, turned)
    received = swap(to_send)
    own = own_product(turned, carried, square)
    selected, variances = finish(own, received)
    return selected, variances.reshape(ROWS)


def solution(mesh):
    placed = (P(AXES, None), P(AXES, None), P(), P(), P("front", None))
    return jax.shard_map(
        on_device,
        mesh=mesh,
        in_specs=placed,
        out_specs=(P(AXES, None), P(AXES)),
        check_vma=False,
    )
```

```python
import jax
import jax.numpy as jnp
import numpy as np
from jax import lax
from jax.experimental import pallas as pl
from jax.experimental.pallas import tpu as pltpu
from jax.sharding import PartitionSpec as P

AXES = ("front", "panel")
BLOCK = 128
STRIP = 32
NABOVE = 16
HALF = NABOVE // 2
SIDE = 1024
ROWS = SIDE // 2
F32 = jnp.float32
BF16 = jnp.bfloat16
VMEM = pl.BlockSpec(memory_space=pltpu.VMEM)
HBM = pl.BlockSpec(memory_space=pltpu.HBM)
ANY = pl.BlockSpec(memory_space=pl.ANY)
SMEM = pl.BlockSpec(memory_space=pltpu.SMEM)
MIB = 1024 * 1024


def params(mib):
    return pltpu.CompilerParams(vmem_limit_bytes=mib * MIB)


def cost(macs, moved):
    return pl.CostEstimate(flops=2 * macs, bytes_accessed=moved, transcendentals=0)


def dot(a, b):
    return jnp.dot(a, b, preferred_element_type=F32)


def dot_tn(a, b):
    return lax.dot_general(a, b, (((0,), (0,)), ((), ())), preferred_element_type=F32)


def split(x):
    hi = x.astype(BF16)
    return hi, (x - hi.astype(F32)).astype(BF16)


def spread(bits, step):
    return step * ((((bits >> 2) & 1) << 4) | (((bits >> 1) & 1) << 2) | (bits & 1))


def steps_of(core):
    return ((1, 3), (3, 1))[core]


def lowest(group, step):
    if step == 1:
        return group & 0b101010
    return group ^ (3 * ((group >> 1) & 0b010101))


def cubes(phase):
    out = []
    for core in range(2):
        step = steps_of(core)[phase]
        for first in range(64):
            if lowest(first, step) == first:
                out.append([(first ^ spread(bits, step)) * 2 + core for bits in range(8)])
    return out


def gather_cube(parts, phase):
    return lax.all_to_all(
        parts, AXES, split_axis=0, concat_axis=0, tiled=True, axis_index_groups=cubes(phase)
    )


def across(x, bits):
    pairs = []
    for group in range(64):
        for core in range(2):
            step = steps_of(core)[1]
            pairs.append((group * 2 + core, (group ^ spread(bits, step)) * 2 + core))
    return lax.ppermute(x, AXES, pairs)


def pick_kernel(slots_hbm, strips_hbm, out_ref, slots_ref, held_ref, sems):
    core, group = lax.axis_index("panel"), lax.axis_index("front")
    table = pltpu.make_async_copy(slots_hbm, slots_ref, sems.at[0])
    fetch = pltpu.make_async_copy(strips_hbm, held_ref, sems.at[1])
    table.start()
    fetch.start()
    table.wait()
    fetch.wait()
    for slot in range(NABOVE):
        row = slots_ref[slot, group] // 64 - core * HALF

        @pl.when((row >= 0) & (row < HALF))
        def _():
            strip = held_ref[slot * STRIP : (slot + 1) * STRIP, :]
            for copy in range(8):
                at = pl.multiple_of(copy * HALF * STRIP + row * STRIP, STRIP)
                out_ref[pl.ds(at, STRIP), :] = strip


def pick_strips(slots, strips):
    return pl.pallas_call(
        pick_kernel,
        out_shape=jax.ShapeDtypeStruct((8 * HALF * STRIP, BLOCK), BF16),
        in_specs=[HBM, HBM],
        out_specs=VMEM,
        scratch_shapes=[
            pltpu.SMEM((NABOVE, 64), jnp.int32),
            pltpu.VMEM((NABOVE * STRIP, BLOCK), BF16),
            pltpu.SemaphoreType.DMA((2,)),
        ],
        compiler_params=params(4),
        cost_estimate=cost(0, 1 << 20),
        name="pick_strips",
    )(*(pltpu.with_memory_space_constraint(x, pltpu.HBM) for x in (slots, strips)))


def solve_kernel(
    mine_hbm, other_hbm, coupling_hbm, after_ref, hi_out, lo_out, wide_out,
    hi_ref, lo_ref, low_ref, coupling_ref, wide_ref, sems,
):
    core = lax.axis_index("panel")
    mine, other = (pl.ds(pl.multiple_of(half * ROWS, ROWS), ROWS) for half in (core, 1 - core))
    fetches = [
        pltpu.make_async_copy(mine_hbm, low_ref.at[mine], sems.at[0]),
        pltpu.make_async_copy(other_hbm, low_ref.at[other], sems.at[1]),
        pltpu.make_async_copy(coupling_hbm, coupling_ref, sems.at[2]),
    ]
    for fetch in fetches:
        fetch.start()
    hi_ref[...] = jnp.zeros_like(hi_ref)
    lo_ref[...] = jnp.zeros_like(lo_ref)
    fetches[0].wait()
    fetches[1].wait()
    row = lax.broadcasted_iota(jnp.int32, (BLOCK, BLOCK), 0)
    col = lax.broadcasted_iota(jnp.int32, (BLOCK, BLOCK), 1)
    differ = row ^ col
    below = row > col
    factors, inverses = [], []
    for b in range(8):
        at = slice(b * BLOCK, (b + 1) * BLOCK)
        factor = low_ref[at, at].astype(F32)
        diag = jnp.where(row == col, factor, 0.0)
        by_row = 1.0 / jnp.sum(diag, axis=1, keepdims=True)
        by_col = 1.0 / jnp.sum(diag, axis=0, keepdims=True)
        next_to = jnp.where(below & (differ < 2), factor, 0.0)
        inverses.append(jnp.where(row == col, by_row, 0.0) - by_row * next_to * by_col)
        factors.append(factor)
    size = 2
    while size < BLOCK:
        mask = below & (differ >= size) & (differ < 2 * size)
        for b in range(8):
            hi, lo = split(inverses[b])
            corner = jnp.where(mask, factors[b], 0.0).astype(BF16)
            both = dot(corner, jnp.concatenate([hi, lo], axis=1))
            t_hi, t_lo = split(both[:, :BLOCK] + both[:, BLOCK:])
            stacked = jnp.concatenate(
                [
                    jnp.concatenate([t_hi, t_lo], axis=1),
                    jnp.concatenate([t_hi, jnp.zeros_like(t_hi)], axis=1),
                ],
                axis=0,
            )
            both = dot(jnp.concatenate([hi, lo], axis=1), stacked)
            inverses[b] = inverses[b] - (both[:, :BLOCK] + both[:, BLOCK:])
        size *= 2
    for b in range(8):
        at = slice(b * BLOCK, (b + 1) * BLOCK)
        hi_ref[at, at], lo_ref[at, at] = split(inverses[b])
    while size < SIDE:
        for start in range(0, SIDE, 2 * size):
            first, second = slice(start, start + size), slice(start + size, start + 2 * size)
            corner = low_ref[second, first]
            t_hi, t_lo = split(dot(corner, hi_ref[first, first]) + dot(corner, lo_ref[first, first]))
            hi, lo = hi_ref[second, second], lo_ref[second, second]
            hi_ref[second, first], lo_ref[second, first] = split(
                -(dot(hi, t_hi) + dot(hi, t_lo) + dot(lo, t_hi))
            )
        size *= 2
    copies = [
        pltpu.make_async_copy(hi_ref, hi_out, sems.at[3]),
        pltpu.make_async_copy(lo_ref, lo_out, sems.at[4]),
    ]
    for copy in copies:
        copy.start()
    fetches[2].wait()
    tile = 256
    for n in range(0, SIDE, tile):
        columns = slice(n, n + tile)
        wide_ref[:, columns] = dot(coupling_ref[:, n:], hi_ref[n:, columns]).astype(BF16)
        copies.append(
            pltpu.make_async_copy(wide_ref.at[:, columns], wide_out.at[:, columns], sems.at[5 + n // tile])
        )
        copies[-1].start()
    for copy in copies:
        copy.wait()


def solve(mine, other, coupling, after):
    full = jax.ShapeDtypeStruct((SIDE, SIDE), BF16)
    return pl.pallas_call(
        solve_kernel,
        out_shape=(full, full, full),
        in_specs=[HBM, HBM, HBM, ANY],
        out_specs=(HBM, HBM, HBM),
        scratch_shapes=[pltpu.VMEM((SIDE, SIDE), BF16)] * 5 + [pltpu.SemaphoreType.DMA((9,))],
        compiler_params=params(60),
        cost_estimate=cost(4 << 30, 12 << 20),
        name="solve",
    )(
        pltpu.with_memory_space_constraint(mine, pltpu.HBM),
        other,
        pltpu.with_memory_space_constraint(coupling, pltpu.HBM),
        after,
    )


def square_kernel(hi_ref, lo_ref, x_ref, y_ref, z_ref, square_ref):
    mine = pl.ds(pl.multiple_of(lax.axis_index("panel") * ROWS, ROWS), ROWS)
    tile = 256
    for n in range(0, SIDE, tile):
        columns = slice(n, n + tile)
        hi, lo = hi_ref[n:, columns], lo_ref[n:, columns]
        left = hi_ref[n:, mine]
        square_ref[:, columns] = dot_tn(left, hi) + dot_tn(left, lo) + dot_tn(lo_ref[n:, mine], hi)


def make_square(hi, lo, after):
    return pl.pallas_call(
        square_kernel,
        out_shape=jax.ShapeDtypeStruct((ROWS, SIDE), F32),
        in_specs=[VMEM, VMEM, ANY, ANY, ANY],
        out_specs=VMEM,
        compiler_params=params(10),
        cost_estimate=cost(1 << 20, 1 << 16),
        name="make_square",
    )(hi, lo, *after)


def turn_kernel(list_ref, slots_ref, mine_ref, other_ref, x_ref, y_ref, z_ref, square_ref, out_ref, table_ref):
    core, group = lax.axis_index("panel"), lax.axis_index("front")
    ids = slots_ref[...]
    rows = [
        jnp.sum(jnp.where((ids >> 6) == core * HALF + row, ids & 63, 0), axis=0, keepdims=True)
        for row in range(HALF)
    ]
    places = jnp.concatenate(rows, axis=0)
    column = jnp.full(places.shape, NABOVE, jnp.int32)
    for a in range(NABOVE):
        column = jnp.where((places >> 2) == list_ref[a, group], a ^ (core * HALF), column)
    row = lax.broadcasted_iota(jnp.int32, places.shape, 0)
    table_ref[...] = column * SIDE + row * BLOCK + (places & 3) * STRIP
    out_ref[...] = jnp.zeros_like(out_ref)
    for a in range(NABOVE):
        owner, at = a // HALF, (a % HALF) * BLOCK
        row = list_ref[a, group] - core * HALF
        columns = pl.ds(pl.multiple_of(jnp.clip(row, 0, HALF - 1) * BLOCK, BLOCK), BLOCK)
        wanted = (row >= 0) & (row < HALF) & (list_ref[a, group] >= 0)

        @pl.when(wanted & (core == owner))
        def _():
            out_ref[:, columns] = mine_ref[at : at + BLOCK, :].astype(F32).T.astype(BF16)

        @pl.when(wanted & (core != owner))
        def _():
            out_ref[:, columns] = other_ref[at : at + BLOCK, :].astype(F32).T.astype(BF16)


def turn_wide(lists, slots, mine, other, after):
    return pl.pallas_call(
        turn_kernel,
        out_shape=(
            jax.ShapeDtypeStruct((SIDE, SIDE), BF16),
            jax.ShapeDtypeStruct((HALF, 64), jnp.int32),
        ),
        in_specs=[SMEM, VMEM, VMEM, VMEM, ANY, ANY, ANY, ANY],
        out_specs=(VMEM, VMEM),
        compiler_params=params(12),
        cost_estimate=cost(1 << 20, 1 << 16),
        name="turn_wide",
    )(lists, slots, mine, other, *after)


def place_strips(table_ref, sigma_ref, strips_ref, bits):
    core, group = lax.axis_index("panel"), lax.axis_index("front")
    first, second = jnp.where(core == 0, 1, 3), jnp.where(core == 0, 3, 1)
    middle = group ^ spread(bits, second)
    start = jnp.where(first == 1, middle & 0b101010, middle ^ (3 * ((middle >> 1) & 0b010101)))

    @pl.loop(0, 8)
    def _(n):
        source = start ^ spread(n, first)
        for row in range(HALF):
            to = pl.multiple_of(table_ref[row, source], STRIP)
            at = pl.multiple_of(n * HALF * STRIP + row * STRIP, STRIP)
            sigma_ref[pl.ds(to, STRIP), :] = strips_ref[pl.ds(at, STRIP), :]


def sigma_kernel(list_ref, table_ref, *refs):
    strips_refs, sigma_ref = refs[:7], refs[7]
    core, group = lax.axis_index("panel"), lax.axis_index("front")
    for a in range(NABOVE):
        column = pl.multiple_of((a ^ (core * HALF)) * SIDE, SIDE)

        @pl.when(list_ref[a, group] < 0)
        def _():
            sigma_ref[pl.ds(column, SIDE), :] = jnp.zeros((SIDE, BLOCK), BF16)

    for bits in range(7):
        place_strips(table_ref, sigma_ref, strips_refs[bits], bits)


SIGMA = jax.ShapeDtypeStruct(((NABOVE + 1) * SIDE, BLOCK), BF16)


def make_sigma(lists, table, strips):
    return pl.pallas_call(
        sigma_kernel,
        out_shape=SIGMA,
        in_specs=[SMEM, SMEM] + [VMEM] * 7,
        out_specs=VMEM,
        compiler_params=params(12),
        cost_estimate=cost(1 << 20, 1 << 16),
        name="make_sigma",
    )(lists, table, *strips)


def carry_kernel(
    table_ref, sigma_in_ref, strips_ref, mine_ref, other_ref, turned_ref, carried_ref, send_ref, sigma_ref
):
    core = lax.axis_index("panel")
    place_strips(table_ref, sigma_ref, strips_ref, 7)

    def sigma(at):
        blocks = [sigma_ref[c * SIDE : (c + 1) * SIDE, :] for c in range(at, at + HALF)]
        return jnp.concatenate(blocks, axis=1)

    tile = 256
    for n in range(0, SIDE, tile):
        columns = slice(n, n + tile)
        carried_ref[:, columns] = (
            dot(sigma(0), mine_ref[:, columns]) + dot(sigma(HALF), other_ref[:, columns])
        ).astype(BF16)
    theirs = pl.ds(pl.multiple_of((1 - core) * ROWS, ROWS), ROWS)
    for n in range(0, SIDE, tile):
        columns = slice(n, n + tile)
        send_ref[:, columns] = dot(turned_ref[theirs, :], carried_ref[:, columns]).astype(BF16)


def carry(table, sigma, last, mine, other, turned):
    return pl.pallas_call(
        carry_kernel,
        out_shape=(
            jax.ShapeDtypeStruct((SIDE, SIDE), BF16),
            jax.ShapeDtypeStruct((ROWS, SIDE), BF16),
            SIGMA,
        ),
        in_specs=[SMEM] + [VMEM] * 5,
        out_specs=(VMEM, VMEM, VMEM),
        input_output_aliases={1: 2},
        compiler_params=params(20),
        cost_estimate=cost(5 << 29, 12 << 20),
        name="carry",
    )(table, sigma, last, mine, other, turned)


def own_kernel(turned_ref, carried_ref, square_ref, out_ref):
    mine = pl.ds(pl.multiple_of(lax.axis_index("panel") * ROWS, ROWS), ROWS)
    tile = 256
    for n in range(0, SIDE, tile):
        columns = slice(n, n + tile)
        out_ref[:, columns] = square_ref[:, columns] + dot(turned_ref[mine, :], carried_ref[:, columns])


def own_product(turned, carried, square):
    return pl.pallas_call(
        own_kernel,
        out_shape=jax.ShapeDtypeStruct((ROWS, SIDE), F32),
        in_specs=[VMEM, VMEM, VMEM],
        out_specs=VMEM,
        compiler_params=params(12),
        cost_estimate=cost(1 << 29, 8 << 20),
        name="own_product",
    )(turned, carried, square)


def finish_kernel(own_ref, received_ref, out_ref, diag_ref):
    out_ref[...] = own_ref[...] + received_ref[...].astype(F32)
    at = lax.axis_index("panel") * ROWS + pl.program_id(0) * BLOCK
    block = out_ref[:, pl.ds(pl.multiple_of(at, BLOCK), BLOCK)]
    row = lax.broadcasted_iota(jnp.int32, (BLOCK, BLOCK), 0)
    col = lax.broadcasted_iota(jnp.int32, (BLOCK, BLOCK), 1)
    diag_ref[...] = jnp.sum(jnp.where(row == col, block, 0.0), axis=0, keepdims=True)


def finish(own, received):
    rows = pl.BlockSpec((BLOCK, SIDE), lambda t: (t, 0))
    return pl.pallas_call(
        finish_kernel,
        grid=(ROWS // BLOCK,),
        out_shape=(
            jax.ShapeDtypeStruct((ROWS, SIDE), F32),
            jax.ShapeDtypeStruct((1, ROWS), F32),
        ),
        in_specs=[rows, rows],
        out_specs=(rows, pl.BlockSpec((1, BLOCK), lambda t: (0, t))),
        compiler_params=params(6),
        cost_estimate=cost(0, 6 << 20),
        name="finish",
    )(own, received)


def swap(x):
    return lax.ppermute(x, "panel", [(0, 1), (1, 0)])


def on_device(sep_factor, coup_factor, coup_list, slot_tiles, anc_tiles):
    lists, slots = coup_list.T, slot_tiles.T
    sep_other = swap(sep_factor)
    picked = pick_strips(slots, anc_tiles)
    near = gather_cube(picked, 0)
    hi, lo, wide_mine = solve(sep_factor, sep_other, coup_factor, picked)
    near, wide_mine = lax.optimization_barrier((near, wide_mine))
    x, y, z = across(near, 1), across(near, 2), across(near, 4)
    wide_other = swap(wide_mine)
    xy, yz, zx = across(x, 2), across(y, 4), across(z, 1)
    square = make_square(hi, lo, (x, y, z))
    xy, square = lax.optimization_barrier((xy, square))
    turned, table = turn_wide(lists, slots, wide_mine, wide_other, (x, y, z, square))
    sigma = make_sigma(lists, table, (near, x, y, xy, z, zx, yz))
    carried, to_send, _ = carry(table, sigma, across(xy, 4), wide_mine, wide_other, turned)
    received = swap(to_send)
    own = own_product(turned, carried, square)
    selected, variances = finish(own, received)
    return selected, variances.reshape(ROWS)


def solution(mesh):
    placed = (P(AXES, None), P(AXES, None), P(), P(), P("front", None))
    return jax.shard_map(
        on_device,
        mesh=mesh,
        in_specs=placed,
        out_specs=(P(AXES, None), P(AXES)),
        check_vma=False,
    )
```

```python
import jax
import jax.numpy as jnp
import numpy as np
from jax import lax
from jax.experimental import pallas as pl
from jax.experimental.pallas import tpu as pltpu
from jax.sharding import PartitionSpec as P

AXES = ("front", "panel")
BLOCK = 128
STRIP = 32
NABOVE = 16
HALF = NABOVE // 2
SIDE = 1024
ROWS = SIDE // 2
F32 = jnp.float32
BF16 = jnp.bfloat16
VMEM = pl.BlockSpec(memory_space=pltpu.VMEM)
HBM = pl.BlockSpec(memory_space=pltpu.HBM)
ANY = pl.BlockSpec(memory_space=pl.ANY)
SMEM = pl.BlockSpec(memory_space=pltpu.SMEM)
MIB = 1024 * 1024


def params(mib):
    return pltpu.CompilerParams(vmem_limit_bytes=mib * MIB)


def cost(macs, moved):
    return pl.CostEstimate(flops=2 * macs, bytes_accessed=moved, transcendentals=0)


def dot(a, b):
    return jnp.dot(a, b, preferred_element_type=F32)


def dot_tn(a, b):
    return lax.dot_general(a, b, (((0,), (0,)), ((), ())), preferred_element_type=F32)


def split(x):
    hi = x.astype(BF16)
    return hi, (x - hi.astype(F32)).astype(BF16)


def spread(bits, step):
    return step * ((((bits >> 2) & 1) << 4) | (((bits >> 1) & 1) << 2) | (bits & 1))


def steps_of(core):
    return ((1, 3), (3, 1))[core]


def lowest(group, step):
    if step == 1:
        return group & 0b101010
    return group ^ (3 * ((group >> 1) & 0b010101))


def cubes(phase):
    out = []
    for core in range(2):
        step = steps_of(core)[phase]
        for first in range(64):
            if lowest(first, step) == first:
                out.append([(first ^ spread(bits, step)) * 2 + core for bits in range(8)])
    return out


def gather_cube(parts, phase):
    return lax.all_to_all(
        parts, AXES, split_axis=0, concat_axis=0, tiled=True, axis_index_groups=cubes(phase)
    )


def across(x, bits):
    pairs = []
    for group in range(64):
        for core in range(2):
            step = steps_of(core)[1]
            pairs.append((group * 2 + core, (group ^ spread(bits, step)) * 2 + core))
    return lax.ppermute(x, AXES, pairs)


def pick_kernel(slots_hbm, strips_hbm, out_ref, slots_ref, held_ref, sems):
    core, group = lax.axis_index("panel"), lax.axis_index("front")
    table = pltpu.make_async_copy(slots_hbm, slots_ref, sems.at[0])
    fetch = pltpu.make_async_copy(strips_hbm, held_ref, sems.at[1])
    table.start()
    fetch.start()
    table.wait()
    fetch.wait()
    for slot in range(NABOVE):
        row = slots_ref[slot, group] // 64 - core * HALF

        @pl.when((row >= 0) & (row < HALF))
        def _():
            strip = held_ref[slot * STRIP : (slot + 1) * STRIP, :]
            for copy in range(8):
                at = pl.multiple_of(copy * HALF * STRIP + row * STRIP, STRIP)
                out_ref[pl.ds(at, STRIP), :] = strip


def pick_strips(slots, strips):
    return pl.pallas_call(
        pick_kernel,
        out_shape=jax.ShapeDtypeStruct((8 * HALF * STRIP, BLOCK), BF16),
        in_specs=[HBM, HBM],
        out_specs=VMEM,
        scratch_shapes=[
            pltpu.SMEM((NABOVE, 64), jnp.int32),
            pltpu.VMEM((NABOVE * STRIP, BLOCK), BF16),
            pltpu.SemaphoreType.DMA((2,)),
        ],
        compiler_params=params(4),
        cost_estimate=cost(0, 1 << 20),
        name="pick_strips",
    )(*(pltpu.with_memory_space_constraint(x, pltpu.HBM) for x in (slots, strips)))


def solve_kernel(
    mine_hbm, other_hbm, coupling_hbm, after_ref, wide_out, square_out,
    hi_ref, lo_ref, low_ref, coupling_ref, wide_ref, square_ref, sems,
):
    core = lax.axis_index("panel")
    mine, other = (pl.ds(pl.multiple_of(half * ROWS, ROWS), ROWS) for half in (core, 1 - core))
    fetches = [
        pltpu.make_async_copy(mine_hbm, low_ref.at[mine], sems.at[0]),
        pltpu.make_async_copy(other_hbm, low_ref.at[other], sems.at[1]),
        pltpu.make_async_copy(coupling_hbm, coupling_ref, sems.at[2]),
    ]
    for fetch in fetches:
        fetch.start()
    hi_ref[...] = jnp.zeros_like(hi_ref)
    lo_ref[...] = jnp.zeros_like(lo_ref)
    fetches[0].wait()
    fetches[1].wait()
    row = lax.broadcasted_iota(jnp.int32, (BLOCK, BLOCK), 0)
    col = lax.broadcasted_iota(jnp.int32, (BLOCK, BLOCK), 1)
    differ = row ^ col
    below = row > col
    factors, inverses = [], []
    for b in range(8):
        at = slice(b * BLOCK, (b + 1) * BLOCK)
        factor = low_ref[at, at].astype(F32)
        diag = jnp.where(row == col, factor, 0.0)
        by_row = 1.0 / jnp.sum(diag, axis=1, keepdims=True)
        by_col = 1.0 / jnp.sum(diag, axis=0, keepdims=True)
        next_to = jnp.where(below & (differ < 2), factor, 0.0)
        inverses.append(jnp.where(row == col, by_row, 0.0) - by_row * next_to * by_col)
        factors.append(factor)
    size = 2
    while size < BLOCK:
        mask = below & (differ >= size) & (differ < 2 * size)
        for b in range(8):
            hi, lo = split(inverses[b])
            corner = jnp.where(mask, factors[b], 0.0).astype(BF16)
            both = dot(corner, jnp.concatenate([hi, lo], axis=1))
            t_hi, t_lo = split(both[:, :BLOCK] + both[:, BLOCK:])
            stacked = jnp.concatenate(
                [
                    jnp.concatenate([t_hi, t_lo], axis=1),
                    jnp.concatenate([t_hi, jnp.zeros_like(t_hi)], axis=1),
                ],
                axis=0,
            )
            both = dot(jnp.concatenate([hi, lo], axis=1), stacked)
            inverses[b] = inverses[b] - (both[:, :BLOCK] + both[:, BLOCK:])
        size *= 2
    for b in range(8):
        at = slice(b * BLOCK, (b + 1) * BLOCK)
        hi_ref[at, at], lo_ref[at, at] = split(inverses[b])
    while size < SIDE:
        for start in range(0, SIDE, 2 * size):
            first, second = slice(start, start + size), slice(start + size, start + 2 * size)
            corner = low_ref[second, first]
            t_hi, t_lo = split(dot(corner, hi_ref[first, first]) + dot(corner, lo_ref[first, first]))
            hi, lo = hi_ref[second, second], lo_ref[second, second]
            hi_ref[second, first], lo_ref[second, first] = split(
                -(dot(hi, t_hi) + dot(hi, t_lo) + dot(lo, t_hi))
            )
        size *= 2
    fetches[2].wait()
    tile = 256
    copies = []
    for n in range(0, SIDE, tile):
        columns = slice(n, n + tile)
        wide_ref[:, columns] = dot(coupling_ref[:, n:], hi_ref[n:, columns]).astype(BF16)
        copies.append(
            pltpu.make_async_copy(wide_ref.at[:, columns], wide_out.at[:, columns], sems.at[3 + n // tile])
        )
        copies[-1].start()
    for n in range(0, SIDE, tile):
        columns = slice(n, n + tile)
        square_ref[:, columns] = dot_tn(hi_ref[n:, mine], hi_ref[n:, columns])
        copies.append(
            pltpu.make_async_copy(square_ref.at[:, columns], square_out.at[:, columns], sems.at[7 + n // tile])
        )
        copies[-1].start()
    for copy in copies:
        copy.wait()


def solve(mine, other, coupling, after):
    return pl.pallas_call(
        solve_kernel,
        out_shape=(
            jax.ShapeDtypeStruct((SIDE, SIDE), BF16),
            jax.ShapeDtypeStruct((ROWS, SIDE), F32),
        ),
        in_specs=[HBM, HBM, HBM, ANY],
        out_specs=(HBM, HBM),
        scratch_shapes=[pltpu.VMEM((SIDE, SIDE), BF16)] * 5
        + [pltpu.VMEM((ROWS, SIDE), F32), pltpu.SemaphoreType.DMA((11,))],
        compiler_params=params(58),
        cost_estimate=cost(4 << 30, 12 << 20),
        name="solve",
    )(
        pltpu.with_memory_space_constraint(mine, pltpu.HBM),
        other,
        pltpu.with_memory_space_constraint(coupling, pltpu.HBM),
        after,
    )


def turn_kernel(list_ref, slots_ref, mine_ref, other_ref, x_ref, y_ref, z_ref, out_ref, table_ref):
    core, group = lax.axis_index("panel"), lax.axis_index("front")
    ids = slots_ref[...]
    rows = [
        jnp.sum(jnp.where((ids >> 6) == core * HALF + row, ids & 63, 0), axis=0, keepdims=True)
        for row in range(HALF)
    ]
    places = jnp.concatenate(rows, axis=0)
    column = jnp.full(places.shape, NABOVE, jnp.int32)
    for a in range(NABOVE):
        column = jnp.where((places >> 2) == list_ref[a, group], a ^ (core * HALF), column)
    row = lax.broadcasted_iota(jnp.int32, places.shape, 0)
    table_ref[...] = column * SIDE + row * BLOCK + (places & 3) * STRIP
    out_ref[...] = jnp.zeros_like(out_ref)
    for a in range(NABOVE):
        owner, at = a // HALF, (a % HALF) * BLOCK
        row = list_ref[a, group] - core * HALF
        columns = pl.ds(pl.multiple_of(jnp.clip(row, 0, HALF - 1) * BLOCK, BLOCK), BLOCK)
        wanted = (row >= 0) & (row < HALF) & (list_ref[a, group] >= 0)

        @pl.when(wanted & (core == owner))
        def _():
            out_ref[:, columns] = mine_ref[at : at + BLOCK, :].astype(F32).T.astype(BF16)

        @pl.when(wanted & (core != owner))
        def _():
            out_ref[:, columns] = other_ref[at : at + BLOCK, :].astype(F32).T.astype(BF16)


def turn_wide(lists, slots, mine, other, after):
    return pl.pallas_call(
        turn_kernel,
        out_shape=(
            jax.ShapeDtypeStruct((SIDE, SIDE), BF16),
            jax.ShapeDtypeStruct((HALF, 64), jnp.int32),
        ),
        in_specs=[SMEM, VMEM, VMEM, VMEM, ANY, ANY, ANY],
        out_specs=(VMEM, VMEM),
        compiler_params=params(12),
        cost_estimate=cost(1 << 20, 1 << 16),
        name="turn_wide",
    )(lists, slots, mine, other, *after)


def place_strips(table_ref, sigma_ref, strips_ref, bits):
    core, group = lax.axis_index("panel"), lax.axis_index("front")
    first, second = jnp.where(core == 0, 1, 3), jnp.where(core == 0, 3, 1)
    middle = group ^ spread(bits, second)
    start = jnp.where(first == 1, middle & 0b101010, middle ^ (3 * ((middle >> 1) & 0b010101)))

    @pl.loop(0, 8)
    def _(n):
        source = start ^ spread(n, first)
        for row in range(HALF):
            to = pl.multiple_of(table_ref[row, source], STRIP)
            at = pl.multiple_of(n * HALF * STRIP + row * STRIP, STRIP)
            sigma_ref[pl.ds(to, STRIP), :] = strips_ref[pl.ds(at, STRIP), :]


def sigma_kernel(list_ref, table_ref, *refs):
    strips_refs, sigma_ref = refs[:7], refs[7]
    core, group = lax.axis_index("panel"), lax.axis_index("front")
    for a in range(NABOVE):
        column = pl.multiple_of((a ^ (core * HALF)) * SIDE, SIDE)

        @pl.when(list_ref[a, group] < 0)
        def _():
            sigma_ref[pl.ds(column, SIDE), :] = jnp.zeros((SIDE, BLOCK), BF16)

    for bits in range(7):
        place_strips(table_ref, sigma_ref, strips_refs[bits], bits)


SIGMA = jax.ShapeDtypeStruct(((NABOVE + 1) * SIDE, BLOCK), BF16)


def make_sigma(lists, table, strips):
    return pl.pallas_call(
        sigma_kernel,
        out_shape=SIGMA,
        in_specs=[SMEM, SMEM] + [VMEM] * 7,
        out_specs=VMEM,
        compiler_params=params(12),
        cost_estimate=cost(1 << 20, 1 << 16),
        name="make_sigma",
    )(lists, table, *strips)


def carry_kernel(
    table_ref, sigma_in_ref, strips_ref, mine_ref, other_ref, turned_ref, carried_ref, send_ref, sigma_ref
):
    core = lax.axis_index("panel")
    place_strips(table_ref, sigma_ref, strips_ref, 7)

    def sigma(at):
        blocks = [sigma_ref[c * SIDE : (c + 1) * SIDE, :] for c in range(at, at + HALF)]
        return jnp.concatenate(blocks, axis=1)

    tile = 256
    for n in range(0, SIDE, tile):
        columns = slice(n, n + tile)
        carried_ref[:, columns] = (
            dot(sigma(0), mine_ref[:, columns]) + dot(sigma(HALF), other_ref[:, columns])
        ).astype(BF16)
    theirs = pl.ds(pl.multiple_of((1 - core) * ROWS, ROWS), ROWS)
    for n in range(0, SIDE, tile):
        columns = slice(n, n + tile)
        send_ref[:, columns] = dot(turned_ref[theirs, :], carried_ref[:, columns]).astype(BF16)


def carry(table, sigma, last, mine, other, turned):
    return pl.pallas_call(
        carry_kernel,
        out_shape=(
            jax.ShapeDtypeStruct((SIDE, SIDE), BF16),
            jax.ShapeDtypeStruct((ROWS, SIDE), BF16),
            SIGMA,
        ),
        in_specs=[SMEM] + [VMEM] * 5,
        out_specs=(VMEM, VMEM, VMEM),
        input_output_aliases={1: 2},
        compiler_params=params(20),
        cost_estimate=cost(5 << 29, 12 << 20),
        name="carry",
    )(table, sigma, last, mine, other, turned)


def own_kernel(turned_ref, carried_ref, square_ref, out_ref):
    mine = pl.ds(pl.multiple_of(lax.axis_index("panel") * ROWS, ROWS), ROWS)
    tile = 256
    for n in range(0, SIDE, tile):
        columns = slice(n, n + tile)
        out_ref[:, columns] = square_ref[:, columns] + dot(turned_ref[mine, :], carried_ref[:, columns])


def own_product(turned, carried, square):
    return pl.pallas_call(
        own_kernel,
        out_shape=jax.ShapeDtypeStruct((ROWS, SIDE), F32),
        in_specs=[VMEM, VMEM, VMEM],
        out_specs=VMEM,
        compiler_params=params(12),
        cost_estimate=cost(1 << 29, 8 << 20),
        name="own_product",
    )(turned, carried, square)


def finish_kernel(own_ref, received_ref, out_ref, diag_ref):
    out_ref[...] = own_ref[...] + received_ref[...].astype(F32)
    at = lax.axis_index("panel") * ROWS + pl.program_id(0) * BLOCK
    block = out_ref[:, pl.ds(pl.multiple_of(at, BLOCK), BLOCK)]
    row = lax.broadcasted_iota(jnp.int32, (BLOCK, BLOCK), 0)
    col = lax.broadcasted_iota(jnp.int32, (BLOCK, BLOCK), 1)
    diag_ref[...] = jnp.sum(jnp.where(row == col, block, 0.0), axis=0, keepdims=True)


def finish(own, received):
    rows = pl.BlockSpec((BLOCK, SIDE), lambda t: (t, 0))
    return pl.pallas_call(
        finish_kernel,
        grid=(ROWS // BLOCK,),
        out_shape=(
            jax.ShapeDtypeStruct((ROWS, SIDE), F32),
            jax.ShapeDtypeStruct((1, ROWS), F32),
        ),
        in_specs=[rows, rows],
        out_specs=(rows, pl.BlockSpec((1, BLOCK), lambda t: (0, t))),
        compiler_params=params(6),
        cost_estimate=cost(0, 6 << 20),
        name="finish",
    )(own, received)


def swap(x):
    return lax.ppermute(x, "panel", [(0, 1), (1, 0)])


def on_device(sep_factor, coup_factor, coup_list, slot_tiles, anc_tiles):
    lists, slots = coup_list.T, slot_tiles.T
    sep_other = swap(sep_factor)
    picked = pick_strips(slots, anc_tiles)
    near = gather_cube(picked, 0)
    wide_mine, square = solve(sep_factor, sep_other, coup_factor, picked)
    near, wide_mine = lax.optimization_barrier((near, wide_mine))
    x, y, z = across(near, 1), across(near, 2), across(near, 4)
    wide_other = swap(wide_mine)
    xy, yz, zx = across(x, 2), across(y, 4), across(z, 1)
    turned, table = turn_wide(lists, slots, wide_mine, wide_other, (x, y, z))
    sigma = make_sigma(lists, table, (near, x, y, xy, z, zx, yz))
    carried, to_send, _ = carry(table, sigma, across(xy, 4), wide_mine, wide_other, turned)
    received = swap(to_send)
    own = own_product(turned, carried, square)
    selected, variances = finish(own, received)
    return selected, variances.reshape(ROWS)


def solution(mesh):
    placed = (P(AXES, None), P(AXES, None), P(), P(), P("front", None))
    return jax.shard_map(
        on_device,
        mesh=mesh,
        in_specs=placed,
        out_specs=(P(AXES, None), P(AXES)),
        check_vma=False,
    )
```

```python
import jax
import jax.numpy as jnp
import numpy as np
from jax import lax
from jax.experimental import pallas as pl
from jax.experimental.pallas import tpu as pltpu
from jax.sharding import PartitionSpec as P

AXES = ("front", "panel")
BLOCK = 128
STRIP = 32
NABOVE = 16
HALF = NABOVE // 2
SIDE = 1024
ROWS = SIDE // 2
F32 = jnp.float32
BF16 = jnp.bfloat16
VMEM = pl.BlockSpec(memory_space=pltpu.VMEM)
HBM = pl.BlockSpec(memory_space=pltpu.HBM)
ANY = pl.BlockSpec(memory_space=pl.ANY)
SMEM = pl.BlockSpec(memory_space=pltpu.SMEM)
MIB = 1024 * 1024


def params(mib):
    return pltpu.CompilerParams(vmem_limit_bytes=mib * MIB)


def cost(macs, moved):
    return pl.CostEstimate(flops=2 * macs, bytes_accessed=moved, transcendentals=0)


def dot(a, b):
    return jnp.dot(a, b, preferred_element_type=F32)


def dot_tn(a, b):
    return lax.dot_general(a, b, (((0,), (0,)), ((), ())), preferred_element_type=F32)


def split(x):
    hi = x.astype(BF16)
    return hi, (x - hi.astype(F32)).astype(BF16)


def spread(bits, step):
    return step * ((((bits >> 2) & 1) << 4) | (((bits >> 1) & 1) << 2) | (bits & 1))


def steps_of(core):
    return ((1, 3), (3, 1))[core]


def lowest(group, step):
    if step == 1:
        return group & 0b101010
    return group ^ (3 * ((group >> 1) & 0b010101))


def cubes(phase):
    out = []
    for core in range(2):
        step = steps_of(core)[phase]
        for first in range(64):
            if lowest(first, step) == first:
                out.append([(first ^ spread(bits, step)) * 2 + core for bits in range(8)])
    return out


def gather_cube(parts, phase):
    return lax.all_to_all(
        parts, AXES, split_axis=0, concat_axis=0, tiled=True, axis_index_groups=cubes(phase)
    )


def across(x, bits):
    pairs = []
    for group in range(64):
        for core in range(2):
            step = steps_of(core)[1]
            pairs.append((group * 2 + core, (group ^ spread(bits, step)) * 2 + core))
    return lax.ppermute(x, AXES, pairs)


def pick_kernel(slots_hbm, lists_hbm, strips_hbm, out_ref, table_ref, slots_ref, list_ref, ids_ref, held_ref, sems):
    core, group = lax.axis_index("panel"), lax.axis_index("front")
    fetches = [
        pltpu.make_async_copy(slots_hbm, slots_ref, sems.at[0]),
        pltpu.make_async_copy(strips_hbm, held_ref, sems.at[1]),
        pltpu.make_async_copy(lists_hbm, list_ref, sems.at[2]),
        pltpu.make_async_copy(slots_hbm, ids_ref, sems.at[3]),
    ]
    for fetch in fetches:
        fetch.start()
    for fetch in fetches:
        fetch.wait()
    for slot in range(NABOVE):
        row = slots_ref[slot, group] // 64 - core * HALF

        @pl.when((row >= 0) & (row < HALF))
        def _():
            strip = held_ref[slot * STRIP : (slot + 1) * STRIP, :]
            for copy in range(8):
                at = pl.multiple_of(copy * HALF * STRIP + row * STRIP, STRIP)
                out_ref[pl.ds(at, STRIP), :] = strip

    ids = ids_ref[...]
    rows = [
        jnp.sum(jnp.where((ids >> 6) == core * HALF + row, ids & 63, 0), axis=0, keepdims=True)
        for row in range(HALF)
    ]
    places = jnp.concatenate(rows, axis=0)
    column = jnp.full(places.shape, NABOVE, jnp.int32)
    for a in range(NABOVE):
        column = jnp.where((places >> 2) == list_ref[a, group], a ^ (core * HALF), column)
    row = lax.broadcasted_iota(jnp.int32, places.shape, 0)
    table_ref[...] = column * SIDE + row * BLOCK + (places & 3) * STRIP


def pick_strips(slots, lists, strips):
    return pl.pallas_call(
        pick_kernel,
        out_shape=(
            jax.ShapeDtypeStruct((8 * HALF * STRIP, BLOCK), BF16),
            jax.ShapeDtypeStruct((HALF, 64), jnp.int32),
        ),
        in_specs=[HBM, HBM, HBM],
        out_specs=(VMEM, VMEM),
        scratch_shapes=[
            pltpu.SMEM((NABOVE, 64), jnp.int32),
            pltpu.SMEM((NABOVE, 64), jnp.int32),
            pltpu.VMEM((NABOVE, 64), jnp.int32),
            pltpu.VMEM((NABOVE * STRIP, BLOCK), BF16),
            pltpu.SemaphoreType.DMA((4,)),
        ],
        compiler_params=params(4),
        cost_estimate=cost(0, 1 << 20),
        name="pick_strips",
    )(*(pltpu.with_memory_space_constraint(x, pltpu.HBM) for x in (slots, lists, strips)))


def blocks_kernel(mine_ref, other_ref, after_ref, hi_ref, lo_ref, low_ref):
    core = lax.axis_index("panel")
    low_ref[pl.ds(pl.multiple_of(core * ROWS, ROWS), ROWS), :] = mine_ref[...]
    low_ref[pl.ds(pl.multiple_of((1 - core) * ROWS, ROWS), ROWS), :] = other_ref[...]
    row = lax.broadcasted_iota(jnp.int32, (BLOCK, BLOCK), 0)
    col = lax.broadcasted_iota(jnp.int32, (BLOCK, BLOCK), 1)
    differ = row ^ col
    below = row > col
    factors, inverses = [], []
    for b in range(8):
        at = slice(b * BLOCK, (b + 1) * BLOCK)
        factor = low_ref[at, at].astype(F32)
        diag = jnp.where(row == col, factor, 0.0)
        by_row = 1.0 / jnp.sum(diag, axis=1, keepdims=True)
        by_col = 1.0 / jnp.sum(diag, axis=0, keepdims=True)
        next_to = jnp.where(below & (differ < 2), factor, 0.0)
        inverses.append(jnp.where(row == col, by_row, 0.0) - by_row * next_to * by_col)
        factors.append(factor)
    size = 2
    while size < BLOCK:
        mask = below & (differ >= size) & (differ < 2 * size)
        for b in range(8):
            hi, lo = split(inverses[b])
            corner = jnp.where(mask, factors[b], 0.0).astype(BF16)
            both = dot(corner, jnp.concatenate([hi, lo], axis=1))
            t_hi, t_lo = split(both[:, :BLOCK] + both[:, BLOCK:])
            stacked = jnp.concatenate(
                [
                    jnp.concatenate([t_hi, t_lo], axis=1),
                    jnp.concatenate([t_hi, jnp.zeros_like(t_hi)], axis=1),
                ],
                axis=0,
            )
            both = dot(jnp.concatenate([hi, lo], axis=1), stacked)
            inverses[b] = inverses[b] - (both[:, :BLOCK] + both[:, BLOCK:])
        size *= 2
    for b in range(8):
        at = slice(b * BLOCK, (b + 1) * BLOCK)
        hi_ref[at, :], lo_ref[at, :] = split(inverses[b])


def invert_blocks(mine, other, after):
    slim = jax.ShapeDtypeStruct((SIDE, BLOCK), BF16)
    return pl.pallas_call(
        blocks_kernel,
        out_shape=(
            slim,
            slim,
            jax.ShapeDtypeStruct((SIDE, SIDE), BF16),
        ),
        in_specs=[VMEM, VMEM, ANY],
        out_specs=(VMEM, VMEM, VMEM),
        compiler_params=params(12),
        cost_estimate=cost(1 << 20, 1 << 16),
        name="invert_blocks",
    )(mine, other, after)


def solve_kernel(
    hi_slim_ref, lo_slim_ref, low_ref, coupling_ref, x_ref, y_ref, z_ref, wide_ref, square_ref, hi_ref, lo_ref
):
    mine = pl.ds(pl.multiple_of(lax.axis_index("panel") * ROWS, ROWS), ROWS)
    hi_ref[...] = jnp.zeros_like(hi_ref)
    lo_ref[...] = jnp.zeros_like(lo_ref)
    for b in range(8):
        at = slice(b * BLOCK, (b + 1) * BLOCK)
        hi_ref[at, at], lo_ref[at, at] = hi_slim_ref[at, :], lo_slim_ref[at, :]
    size = BLOCK
    while size < SIDE:
        for start in range(0, SIDE, 2 * size):
            first, second = slice(start, start + size), slice(start + size, start + 2 * size)
            corner = low_ref[second, first]
            t_hi, t_lo = split(dot(corner, hi_ref[first, first]) + dot(corner, lo_ref[first, first]))
            hi, lo = hi_ref[second, second], lo_ref[second, second]
            hi_ref[second, first], lo_ref[second, first] = split(
                -(dot(hi, t_hi) + dot(hi, t_lo) + dot(lo, t_hi))
            )
        size *= 2
    tile = 256
    for n in range(0, SIDE, tile):
        columns = slice(n, n + tile)
        wide_ref[:, columns] = dot(coupling_ref[:, n:], hi_ref[n:, columns]).astype(BF16)
    for n in range(0, SIDE, tile):
        columns = slice(n, n + tile)
        square_ref[:, columns] = dot_tn(hi_ref[n:, mine], hi_ref[n:, columns])


def solve(hi, lo, low, coupling, after):
    return pl.pallas_call(
        solve_kernel,
        out_shape=(
            jax.ShapeDtypeStruct((SIDE, SIDE), BF16),
            jax.ShapeDtypeStruct((ROWS, SIDE), F32),
        ),
        in_specs=[VMEM, VMEM, VMEM, VMEM, ANY, ANY, ANY],
        out_specs=(VMEM, VMEM),
        scratch_shapes=[pltpu.VMEM((SIDE, SIDE), BF16)] * 2,
        compiler_params=params(20),
        cost_estimate=cost(1 << 20, 1 << 16),
        name="solve",
    )(hi, lo, low, coupling, *after)


def turn_kernel(list_ref, mine_ref, other_ref, out_ref):
    core, group = lax.axis_index("panel"), lax.axis_index("front")
    out_ref[...] = jnp.zeros_like(out_ref)
    for a in range(NABOVE):
        owner, at = a // HALF, (a % HALF) * BLOCK
        row = list_ref[a, group] - core * HALF
        columns = pl.ds(pl.multiple_of(jnp.clip(row, 0, HALF - 1) * BLOCK, BLOCK), BLOCK)
        wanted = (row >= 0) & (row < HALF) & (list_ref[a, group] >= 0)

        @pl.when(wanted & (core == owner))
        def _():
            out_ref[:, columns] = mine_ref[at : at + BLOCK, :].astype(F32).T.astype(BF16)

        @pl.when(wanted & (core != owner))
        def _():
            out_ref[:, columns] = other_ref[at : at + BLOCK, :].astype(F32).T.astype(BF16)


def turn_wide(lists, mine, other):
    return pl.pallas_call(
        turn_kernel,
        out_shape=jax.ShapeDtypeStruct((SIDE, SIDE), BF16),
        in_specs=[SMEM, VMEM, VMEM],
        out_specs=VMEM,
        compiler_params=params(12),
        cost_estimate=cost(0, 8 << 20),
        name="turn_wide",
    )(lists, mine, other)


def place_strips(table_ref, sigma_ref, strips_ref, bits):
    core, group = lax.axis_index("panel"), lax.axis_index("front")
    first, second = jnp.where(core == 0, 1, 3), jnp.where(core == 0, 3, 1)
    middle = group ^ spread(bits, second)
    start = jnp.where(first == 1, middle & 0b101010, middle ^ (3 * ((middle >> 1) & 0b010101)))

    @pl.loop(0, 8)
    def _(n):
        source = start ^ spread(n, first)
        for row in range(HALF):
            to = pl.multiple_of(table_ref[row, source], STRIP)
            at = pl.multiple_of(n * HALF * STRIP + row * STRIP, STRIP)
            sigma_ref[pl.ds(to, STRIP), :] = strips_ref[pl.ds(at, STRIP), :]


def sigma_kernel(list_ref, table_ref, *refs):
    strips_refs, sigma_ref = refs[:7], refs[7]
    core, group = lax.axis_index("panel"), lax.axis_index("front")
    for a in range(NABOVE):
        column = pl.multiple_of((a ^ (core * HALF)) * SIDE, SIDE)

        @pl.when(list_ref[a, group] < 0)
        def _():
            sigma_ref[pl.ds(column, SIDE), :] = jnp.zeros((SIDE, BLOCK), BF16)

    for bits in range(7):
        place_strips(table_ref, sigma_ref, strips_refs[bits], bits)


SIGMA = jax.ShapeDtypeStruct(((NABOVE + 1) * SIDE, BLOCK), BF16)


def make_sigma(lists, table, strips):
    return pl.pallas_call(
        sigma_kernel,
        out_shape=SIGMA,
        in_specs=[SMEM, SMEM] + [VMEM] * 7,
        out_specs=VMEM,
        compiler_params=params(12),
        cost_estimate=cost(0, 10 << 20),
        name="make_sigma",
    )(lists, table, *strips)


def carry_kernel(
    table_ref, sigma_in_ref, strips_ref, mine_ref, other_ref, turned_ref, carried_ref, send_ref, sigma_ref
):
    core = lax.axis_index("panel")
    place_strips(table_ref, sigma_ref, strips_ref, 7)

    def sigma(at):
        blocks = [sigma_ref[c * SIDE : (c + 1) * SIDE, :] for c in range(at, at + HALF)]
        return jnp.concatenate(blocks, axis=1)

    tile = 256
    for n in range(0, SIDE, tile):
        columns = slice(n, n + tile)
        carried_ref[:, columns] = (
            dot(sigma(0), mine_ref[:, columns]) + dot(sigma(HALF), other_ref[:, columns])
        ).astype(BF16)
    theirs = pl.ds(pl.multiple_of((1 - core) * ROWS, ROWS), ROWS)
    for n in range(0, SIDE, tile):
        columns = slice(n, n + tile)
        send_ref[:, columns] = dot(turned_ref[theirs, :], carried_ref[:, columns]).astype(BF16)


def carry(table, sigma, last, mine, other, turned):
    return pl.pallas_call(
        carry_kernel,
        out_shape=(
            jax.ShapeDtypeStruct((SIDE, SIDE), BF16),
            jax.ShapeDtypeStruct((ROWS, SIDE), BF16),
            SIGMA,
        ),
        in_specs=[SMEM] + [VMEM] * 5,
        out_specs=(VMEM, VMEM, VMEM),
        input_output_aliases={1: 2},
        compiler_params=params(20),
        cost_estimate=cost(5 << 29, 12 << 20),
        name="carry",
    )(table, sigma, last, mine, other, turned)


def own_kernel(turned_ref, carried_ref, square_ref, out_ref):
    mine = pl.ds(pl.multiple_of(lax.axis_index("panel") * ROWS, ROWS), ROWS)
    tile = 256
    for n in range(0, SIDE, tile):
        columns = slice(n, n + tile)
        out_ref[:, columns] = square_ref[:, columns] + dot(turned_ref[mine, :], carried_ref[:, columns])


def own_product(turned, carried, square):
    return pl.pallas_call(
        own_kernel,
        out_shape=jax.ShapeDtypeStruct((ROWS, SIDE), F32),
        in_specs=[VMEM, VMEM, VMEM],
        out_specs=VMEM,
        compiler_params=params(12),
        cost_estimate=cost(1 << 29, 8 << 20),
        name="own_product",
    )(turned, carried, square)


def finish_kernel(own_ref, received_ref, out_ref, diag_ref):
    out_ref[...] = own_ref[...] + received_ref[...].astype(F32)
    at = lax.axis_index("panel") * ROWS + pl.program_id(0) * BLOCK
    block = out_ref[:, pl.ds(pl.multiple_of(at, BLOCK), BLOCK)]
    row = lax.broadcasted_iota(jnp.int32, (BLOCK, BLOCK), 0)
    col = lax.broadcasted_iota(jnp.int32, (BLOCK, BLOCK), 1)
    diag_ref[...] = jnp.sum(jnp.where(row == col, block, 0.0), axis=0, keepdims=True)


def finish(own, received):
    rows = pl.BlockSpec((BLOCK, SIDE), lambda t: (t, 0))
    return pl.pallas_call(
        finish_kernel,
        grid=(ROWS // BLOCK,),
        out_shape=(
            jax.ShapeDtypeStruct((ROWS, SIDE), F32),
            jax.ShapeDtypeStruct((1, ROWS), F32),
        ),
        in_specs=[rows, rows],
        out_specs=(rows, pl.BlockSpec((1, BLOCK), lambda t: (0, t))),
        compiler_params=params(6),
        cost_estimate=cost(0, 6 << 20),
        name="finish",
    )(own, received)


def swap(x):
    return lax.ppermute(x, "panel", [(0, 1), (1, 0)])


def on_device(sep_factor, coup_factor, coup_list, slot_tiles, anc_tiles):
    lists, slots = coup_list.T, slot_tiles.T
    sep_other = swap(sep_factor)
    picked, table = pick_strips(slots, lists, anc_tiles)
    near = gather_cube(picked, 0)
    hi, lo, low = invert_blocks(sep_factor, sep_other, near)
    x, y, z = across(near, 1), across(near, 2), across(near, 4)
    x, y, z, hi = lax.optimization_barrier((x, y, z, hi))
    xy, yz, zx = across(x, 2), across(y, 4), across(z, 1)
    wide_mine, square = solve(hi, lo, low, coup_factor, (x, y, z))
    xy, yz, zx, wide_mine, square = lax.optimization_barrier((xy, yz, zx, wide_mine, square))
    wide_other = swap(wide_mine)
    turned = turn_wide(lists, wide_mine, wide_other)
    sigma = make_sigma(lists, table, (near, x, y, xy, z, zx, yz))
    carried, to_send, _ = carry(table, sigma, across(xy, 4), wide_mine, wide_other, turned)
    received = swap(to_send)
    own = own_product(turned, carried, square)
    selected, variances = finish(own, received)
    return selected, variances.reshape(ROWS)


def solution(mesh):
    placed = (P(AXES, None), P(AXES, None), P(), P(), P("front", None))
    return jax.shard_map(
        on_device,
        mesh=mesh,
        in_specs=placed,
        out_specs=(P(AXES, None), P(AXES)),
        check_vma=False,
    )
```

```python
import jax
import jax.numpy as jnp
import numpy as np
from jax import lax
from jax.experimental import pallas as pl
from jax.experimental.pallas import tpu as pltpu
from jax.sharding import PartitionSpec as P

AXES = ("front", "panel")
BLOCK = 128
STRIP = 32
NABOVE = 16
HALF = NABOVE // 2
SIDE = 1024
ROWS = SIDE // 2
F32 = jnp.float32
BF16 = jnp.bfloat16
VMEM = pl.BlockSpec(memory_space=pltpu.VMEM)
HBM = pl.BlockSpec(memory_space=pltpu.HBM)
ANY = pl.BlockSpec(memory_space=pl.ANY)
SMEM = pl.BlockSpec(memory_space=pltpu.SMEM)
MIB = 1024 * 1024


def params(mib):
    return pltpu.CompilerParams(vmem_limit_bytes=mib * MIB)


def cost(macs, moved):
    return pl.CostEstimate(flops=2 * macs, bytes_accessed=moved, transcendentals=0)


def dot(a, b):
    return jnp.dot(a, b, preferred_element_type=F32)


def dot_tn(a, b):
    return lax.dot_general(a, b, (((0,), (0,)), ((), ())), preferred_element_type=F32)


def split(x):
    hi = x.astype(BF16)
    return hi, (x - hi.astype(F32)).astype(BF16)


def spread(bits, step):
    return step * ((((bits >> 2) & 1) << 4) | (((bits >> 1) & 1) << 2) | (bits & 1))


def steps_of(core):
    return ((1, 3), (3, 1))[core]


def lowest(group, step):
    if step == 1:
        return group & 0b101010
    return group ^ (3 * ((group >> 1) & 0b010101))


def cubes(phase):
    out = []
    for core in range(2):
        step = steps_of(core)[phase]
        for first in range(64):
            if lowest(first, step) == first:
                out.append([(first ^ spread(bits, step)) * 2 + core for bits in range(8)])
    return out


def gather_cube(parts, phase):
    return lax.all_to_all(
        parts, AXES, split_axis=0, concat_axis=0, tiled=True, axis_index_groups=cubes(phase)
    )


def across(x, bits):
    pairs = []
    for group in range(64):
        for core in range(2):
            step = steps_of(core)[1]
            pairs.append((group * 2 + core, (group ^ spread(bits, step)) * 2 + core))
    return lax.ppermute(x, AXES, pairs)


def pick_kernel(slots_hbm, lists_hbm, strips_hbm, out_ref, table_ref, slots_ref, list_ref, ids_ref, held_ref, sems):
    core, group = lax.axis_index("panel"), lax.axis_index("front")
    fetches = [
        pltpu.make_async_copy(slots_hbm, slots_ref, sems.at[0]),
        pltpu.make_async_copy(strips_hbm, held_ref, sems.at[1]),
        pltpu.make_async_copy(lists_hbm, list_ref, sems.at[2]),
        pltpu.make_async_copy(slots_hbm, ids_ref, sems.at[3]),
    ]
    for fetch in fetches:
        fetch.start()
    for fetch in fetches:
        fetch.wait()
    for slot in range(NABOVE):
        row = slots_ref[slot, group] // 64 - core * HALF

        @pl.when((row >= 0) & (row < HALF))
        def _():
            strip = held_ref[slot * STRIP : (slot + 1) * STRIP, :]
            for copy in range(8):
                at = pl.multiple_of(copy * HALF * STRIP + row * STRIP, STRIP)
                out_ref[pl.ds(at, STRIP), :] = strip

    ids = ids_ref[...]
    rows = [
        jnp.sum(jnp.where((ids >> 6) == core * HALF + row, ids & 63, 0), axis=0, keepdims=True)
        for row in range(HALF)
    ]
    places = jnp.concatenate(rows, axis=0)
    column = jnp.full(places.shape, NABOVE, jnp.int32)
    for a in range(NABOVE):
        column = jnp.where((places >> 2) == list_ref[a, group], a ^ (core * HALF), column)
    row = lax.broadcasted_iota(jnp.int32, places.shape, 0)
    table_ref[...] = column * SIDE + row * BLOCK + (places & 3) * STRIP


def pick_strips(slots, lists, strips):
    return pl.pallas_call(
        pick_kernel,
        out_shape=(
            jax.ShapeDtypeStruct((8 * HALF * STRIP, BLOCK), BF16),
            jax.ShapeDtypeStruct((HALF, 64), jnp.int32),
        ),
        in_specs=[HBM, HBM, HBM],
        out_specs=(VMEM, VMEM),
        scratch_shapes=[
            pltpu.SMEM((NABOVE, 64), jnp.int32),
            pltpu.SMEM((NABOVE, 64), jnp.int32),
            pltpu.VMEM((NABOVE, 64), jnp.int32),
            pltpu.VMEM((NABOVE * STRIP, BLOCK), BF16),
            pltpu.SemaphoreType.DMA((4,)),
        ],
        compiler_params=params(4),
        cost_estimate=cost(0, 1 << 20),
        name="pick_strips",
    )(*(pltpu.with_memory_space_constraint(x, pltpu.HBM) for x in (slots, lists, strips)))


def blocks_kernel(mine_ref, other_ref, after_ref, hi_ref, lo_ref, low_ref):
    core = lax.axis_index("panel")
    low_ref[pl.ds(pl.multiple_of(core * ROWS, ROWS), ROWS), :] = mine_ref[...]
    low_ref[pl.ds(pl.multiple_of((1 - core) * ROWS, ROWS), ROWS), :] = other_ref[...]
    row = lax.broadcasted_iota(jnp.int32, (BLOCK, BLOCK), 0)
    col = lax.broadcasted_iota(jnp.int32, (BLOCK, BLOCK), 1)
    differ = row ^ col
    below = row > col
    factors, inverses = [], []
    for b in range(8):
        at = slice(b * BLOCK, (b + 1) * BLOCK)
        factor = low_ref[at, at].astype(F32)
        diag = jnp.where(row == col, factor, 0.0)
        by_row = 1.0 / jnp.sum(diag, axis=1, keepdims=True)
        by_col = 1.0 / jnp.sum(diag, axis=0, keepdims=True)
        next_to = jnp.where(below & (differ < 2), factor, 0.0)
        inverses.append(jnp.where(row == col, by_row, 0.0) - by_row * next_to * by_col)
        factors.append(factor)
    size = 2
    while size < BLOCK:
        mask = below & (differ >= size) & (differ < 2 * size)
        for b in range(8):
            hi, lo = split(inverses[b])
            corner = jnp.where(mask, factors[b], 0.0).astype(BF16)
            both = dot(corner, jnp.concatenate([hi, lo], axis=1))
            t_hi, t_lo = split(both[:, :BLOCK] + both[:, BLOCK:])
            stacked = jnp.concatenate(
                [
                    jnp.concatenate([t_hi, t_lo], axis=1),
                    jnp.concatenate([t_hi, jnp.zeros_like(t_hi)], axis=1),
                ],
                axis=0,
            )
            both = dot(jnp.concatenate([hi, lo], axis=1), stacked)
            inverses[b] = inverses[b] - (both[:, :BLOCK] + both[:, BLOCK:])
        size *= 2
    for b in range(8):
        at = slice(b * BLOCK, (b + 1) * BLOCK)
        hi_ref[at, :], lo_ref[at, :] = split(inverses[b])


def invert_blocks(mine, other, after):
    slim = jax.ShapeDtypeStruct((SIDE, BLOCK), BF16)
    return pl.pallas_call(
        blocks_kernel,
        out_shape=(
            slim,
            slim,
            jax.ShapeDtypeStruct((SIDE, SIDE), BF16),
        ),
        in_specs=[VMEM, VMEM, ANY],
        out_specs=(VMEM, VMEM, VMEM),
        compiler_params=params(12),
        cost_estimate=cost(1 << 20, 1 << 16),
        name="invert_blocks",
    )(mine, other, after)


def solve_kernel(
    hi_slim_ref, lo_slim_ref, low_ref, coupling_ref, x_ref, y_ref, z_ref, wide_ref, square_ref, hi_ref, lo_ref
):
    mine = pl.ds(pl.multiple_of(lax.axis_index("panel") * ROWS, ROWS), ROWS)
    hi_ref[...] = jnp.zeros_like(hi_ref)
    lo_ref[...] = jnp.zeros_like(lo_ref)
    for b in range(8):
        at = slice(b * BLOCK, (b + 1) * BLOCK)
        hi_ref[at, at], lo_ref[at, at] = hi_slim_ref[at, :], lo_slim_ref[at, :]
    size = BLOCK
    while size < SIDE:
        for start in range(0, SIDE, 2 * size):
            first, second = slice(start, start + size), slice(start + size, start + 2 * size)
            corner = low_ref[second, first]
            t_hi, t_lo = split(dot(corner, hi_ref[first, first]) + dot(corner, lo_ref[first, first]))
            hi, lo = hi_ref[second, second], lo_ref[second, second]
            hi_ref[second, first], lo_ref[second, first] = split(
                -(dot(hi, t_hi) + dot(hi, t_lo) + dot(lo, t_hi))
            )
        size *= 2
    tile = 256
    for n in range(0, SIDE, tile):
        columns = slice(n, n + tile)
        wide_ref[:, columns] = dot(coupling_ref[:, n:], hi_ref[n:, columns]).astype(BF16)
    for n in range(0, SIDE, tile):
        columns = slice(n, n + tile)
        square_ref[:, columns] = dot_tn(hi_ref[n:, mine], hi_ref[n:, columns])


def solve(hi, lo, low, coupling, after):
    return pl.pallas_call(
        solve_kernel,
        out_shape=(
            jax.ShapeDtypeStruct((SIDE, SIDE), BF16),
            jax.ShapeDtypeStruct((ROWS, SIDE), F32),
        ),
        in_specs=[VMEM, VMEM, VMEM, VMEM, ANY, ANY, ANY],
        out_specs=(VMEM, VMEM),
        scratch_shapes=[pltpu.VMEM((SIDE, SIDE), BF16)] * 2,
        compiler_params=params(20),
        cost_estimate=cost(1 << 20, 1 << 16),
        name="solve",
    )(hi, lo, low, coupling, *after)


def turn_kernel(list_ref, mine_ref, other_ref, out_ref):
    core, group = lax.axis_index("panel"), lax.axis_index("front")
    out_ref[...] = jnp.zeros_like(out_ref)
    for a in range(NABOVE):
        owner, at = a // HALF, (a % HALF) * BLOCK
        row = list_ref[a, group] - core * HALF
        columns = pl.ds(pl.multiple_of(jnp.clip(row, 0, HALF - 1) * BLOCK, BLOCK), BLOCK)
        wanted = (row >= 0) & (row < HALF) & (list_ref[a, group] >= 0)

        @pl.when(wanted & (core == owner))
        def _():
            out_ref[:, columns] = mine_ref[at : at + BLOCK, :].astype(F32).T.astype(BF16)

        @pl.when(wanted & (core != owner))
        def _():
            out_ref[:, columns] = other_ref[at : at + BLOCK, :].astype(F32).T.astype(BF16)


def turn_wide(lists, mine, other):
    return pl.pallas_call(
        turn_kernel,
        out_shape=jax.ShapeDtypeStruct((SIDE, SIDE), BF16),
        in_specs=[SMEM, VMEM, VMEM],
        out_specs=VMEM,
        compiler_params=params(12),
        cost_estimate=cost(0, 8 << 20),
        name="turn_wide",
    )(lists, mine, other)


def place_strips(table_ref, sigma_ref, strips_ref, bits):
    core, group = lax.axis_index("panel"), lax.axis_index("front")
    first, second = jnp.where(core == 0, 1, 3), jnp.where(core == 0, 3, 1)
    middle = group ^ spread(bits, second)
    start = jnp.where(first == 1, middle & 0b101010, middle ^ (3 * ((middle >> 1) & 0b010101)))

    @pl.loop(0, 8)
    def _(n):
        source = start ^ spread(n, first)
        for row in range(HALF):
            to = pl.multiple_of(table_ref[row, source], STRIP)
            at = pl.multiple_of(n * HALF * STRIP + row * STRIP, STRIP)
            sigma_ref[pl.ds(to, STRIP), :] = strips_ref[pl.ds(at, STRIP), :]


def sigma_kernel(list_ref, table_ref, *refs):
    strips_refs, sigma_ref = refs[:7], refs[7]
    core, group = lax.axis_index("panel"), lax.axis_index("front")
    for a in range(NABOVE):
        column = pl.multiple_of((a ^ (core * HALF)) * SIDE, SIDE)

        @pl.when(list_ref[a, group] < 0)
        def _():
            sigma_ref[pl.ds(column, SIDE), :] = jnp.zeros((SIDE, BLOCK), BF16)

    for bits in range(7):
        place_strips(table_ref, sigma_ref, strips_refs[bits], bits)


SIGMA = jax.ShapeDtypeStruct(((NABOVE + 1) * SIDE, BLOCK), BF16)


def make_sigma(lists, table, strips):
    return pl.pallas_call(
        sigma_kernel,
        out_shape=SIGMA,
        in_specs=[SMEM, SMEM] + [VMEM] * 7,
        out_specs=VMEM,
        compiler_params=params(12),
        cost_estimate=cost(0, 10 << 20),
        name="make_sigma",
    )(lists, table, *strips)


def carry_kernel(
    table_ref, sigma_in_ref, strips_ref, mine_ref, other_ref, turned_ref, carried_ref, send_ref, sigma_ref
):
    core = lax.axis_index("panel")
    place_strips(table_ref, sigma_ref, strips_ref, 7)

    def sigma(at):
        blocks = [sigma_ref[c * SIDE : (c + 1) * SIDE, :] for c in range(at, at + HALF)]
        return jnp.concatenate(blocks, axis=1)

    tile = 256
    for n in range(0, SIDE, tile):
        columns = slice(n, n + tile)
        carried_ref[:, columns] = (
            dot(sigma(0), mine_ref[:, columns]) + dot(sigma(HALF), other_ref[:, columns])
        ).astype(BF16)
    theirs = pl.ds(pl.multiple_of((1 - core) * ROWS, ROWS), ROWS)
    for n in range(0, SIDE, tile):
        columns = slice(n, n + tile)
        send_ref[:, columns] = dot(turned_ref[theirs, :], carried_ref[:, columns]).astype(BF16)


def carry(table, sigma, last, mine, other, turned):
    return pl.pallas_call(
        carry_kernel,
        out_shape=(
            jax.ShapeDtypeStruct((SIDE, SIDE), BF16),
            jax.ShapeDtypeStruct((ROWS, SIDE), BF16),
            SIGMA,
        ),
        in_specs=[SMEM] + [VMEM] * 5,
        out_specs=(VMEM, VMEM, VMEM),
        input_output_aliases={1: 2},
        compiler_params=params(20),
        cost_estimate=cost(5 << 29, 12 << 20),
        name="carry",
    )(table, sigma, last, mine, other, turned)


def own_kernel(turned_ref, carried_ref, square_ref, out_ref):
    mine = pl.ds(pl.multiple_of(lax.axis_index("panel") * ROWS, ROWS), ROWS)
    tile = 256
    for n in range(0, SIDE, tile):
        columns = slice(n, n + tile)
        out_ref[:, columns] = square_ref[:, columns] + dot(turned_ref[mine, :], carried_ref[:, columns])


def own_product(turned, carried, square):
    return pl.pallas_call(
        own_kernel,
        out_shape=jax.ShapeDtypeStruct((ROWS, SIDE), F32),
        in_specs=[VMEM, VMEM, VMEM],
        out_specs=VMEM,
        compiler_params=params(12),
        cost_estimate=cost(1 << 29, 8 << 20),
        name="own_product",
    )(turned, carried, square)


def finish_kernel(own_ref, received_ref, out_ref, diag_ref):
    out_ref[...] = own_ref[...] + received_ref[...].astype(F32)
    at = lax.axis_index("panel") * ROWS + pl.program_id(0) * BLOCK
    block = out_ref[:, pl.ds(pl.multiple_of(at, BLOCK), BLOCK)]
    row = lax.broadcasted_iota(jnp.int32, (BLOCK, BLOCK), 0)
    col = lax.broadcasted_iota(jnp.int32, (BLOCK, BLOCK), 1)
    diag_ref[...] = jnp.sum(jnp.where(row == col, block, 0.0), axis=0, keepdims=True)


def finish(own, received):
    rows = pl.BlockSpec((BLOCK, SIDE), lambda t: (t, 0))
    return pl.pallas_call(
        finish_kernel,
        grid=(ROWS // BLOCK,),
        out_shape=(
            jax.ShapeDtypeStruct((ROWS, SIDE), F32),
            jax.ShapeDtypeStruct((1, ROWS), F32),
        ),
        in_specs=[rows, rows],
        out_specs=(rows, pl.BlockSpec((1, BLOCK), lambda t: (0, t))),
        compiler_params=params(6),
        cost_estimate=cost(0, 6 << 20),
        name="finish",
    )(own, received)


def swap(x):
    return lax.ppermute(x, "panel", [(0, 1), (1, 0)])


def on_device(sep_factor, coup_factor, coup_list, slot_tiles, anc_tiles):
    lists, slots = coup_list.T, slot_tiles.T
    sep_other = swap(sep_factor)
    picked, table = pick_strips(slots, lists, anc_tiles)
    near = gather_cube(picked, 0)
    hi, lo, low = invert_blocks(sep_factor, sep_other, near)
    x, y, z = across(near, 1), across(near, 2), across(near, 4)
    z, hi = lax.optimization_barrier((z, hi))
    xy, yz, zx = across(x, 2), across(y, 4), across(z, 1)
    wide_mine, square = solve(hi, lo, low, coup_factor, (x, y, z))
    xy, yz, zx, wide_mine, square = lax.optimization_barrier((xy, yz, zx, wide_mine, square))
    wide_other = swap(wide_mine)
    turned = turn_wide(lists, wide_mine, wide_other)
    sigma = make_sigma(lists, table, (near, x, y, xy, z, zx, yz))
    carried, to_send, _ = carry(table, sigma, across(xy, 4), wide_mine, wide_other, turned)
    received = swap(to_send)
    own = own_product(turned, carried, square)
    selected, variances = finish(own, received)
    return selected, variances.reshape(ROWS)


def solution(mesh):
    placed = (P(AXES, None), P(AXES, None), P(), P(), P("front", None))
    return jax.shard_map(
        on_device,
        mesh=mesh,
        in_specs=placed,
        out_specs=(P(AXES, None), P(AXES)),
        check_vma=False,
    )
```

```python
import jax
import jax.numpy as jnp
import numpy as np
from jax import lax
from jax.experimental import pallas as pl
from jax.experimental.pallas import tpu as pltpu
from jax.sharding import PartitionSpec as P

AXES = ("front", "panel")
BLOCK = 128
STRIP = 32
NABOVE = 16
HALF = NABOVE // 2
SIDE = 1024
ROWS = SIDE // 2
F32 = jnp.float32
BF16 = jnp.bfloat16
VMEM = pl.BlockSpec(memory_space=pltpu.VMEM)
HBM = pl.BlockSpec(memory_space=pltpu.HBM)
ANY = pl.BlockSpec(memory_space=pl.ANY)
SMEM = pl.BlockSpec(memory_space=pltpu.SMEM)
MIB = 1024 * 1024


def params(mib):
    return pltpu.CompilerParams(vmem_limit_bytes=mib * MIB)


def cost(macs, moved):
    return pl.CostEstimate(flops=2 * macs, bytes_accessed=moved, transcendentals=0)


def dot(a, b):
    return jnp.dot(a, b, preferred_element_type=F32)


def dot_tn(a, b):
    return lax.dot_general(a, b, (((0,), (0,)), ((), ())), preferred_element_type=F32)


def split(x):
    hi = x.astype(BF16)
    return hi, (x - hi.astype(F32)).astype(BF16)


def spread(bits, step):
    return step * ((((bits >> 2) & 1) << 4) | (((bits >> 1) & 1) << 2) | (bits & 1))


def steps_of(core):
    return ((1, 3), (3, 1))[core]


def lowest(group, step):
    if step == 1:
        return group & 0b101010
    return group ^ (3 * ((group >> 1) & 0b010101))


def cubes(phase):
    out = []
    for core in range(2):
        step = steps_of(core)[phase]
        for first in range(64):
            if lowest(first, step) == first:
                out.append([(first ^ spread(bits, step)) * 2 + core for bits in range(8)])
    return out


def gather_cube(parts, phase):
    return lax.all_to_all(
        parts, AXES, split_axis=0, concat_axis=0, tiled=True, axis_index_groups=cubes(phase)
    )


def across(x, bits):
    pairs = []
    for group in range(64):
        for core in range(2):
            step = steps_of(core)[1]
            pairs.append((group * 2 + core, (group ^ spread(bits, step)) * 2 + core))
    return lax.ppermute(x, AXES, pairs)


def pick_kernel(slots_hbm, lists_hbm, strips_hbm, out_ref, table_ref, slots_ref, list_ref, ids_ref, held_ref, sems):
    core, group = lax.axis_index("panel"), lax.axis_index("front")
    fetches = [
        pltpu.make_async_copy(slots_hbm, slots_ref, sems.at[0]),
        pltpu.make_async_copy(strips_hbm, held_ref, sems.at[1]),
        pltpu.make_async_copy(lists_hbm, list_ref, sems.at[2]),
        pltpu.make_async_copy(slots_hbm, ids_ref, sems.at[3]),
    ]
    for fetch in fetches:
        fetch.start()
    for fetch in fetches:
        fetch.wait()
    for slot in range(NABOVE):
        row = slots_ref[slot, group] // 64 - core * HALF

        @pl.when((row >= 0) & (row < HALF))
        def _():
            strip = held_ref[slot * STRIP : (slot + 1) * STRIP, :]
            for copy in range(8):
                at = pl.multiple_of(copy * HALF * STRIP + row * STRIP, STRIP)
                out_ref[pl.ds(at, STRIP), :] = strip

    ids = ids_ref[...]
    rows = [
        jnp.sum(jnp.where((ids >> 6) == core * HALF + row, ids & 63, 0), axis=0, keepdims=True)
        for row in range(HALF)
    ]
    places = jnp.concatenate(rows, axis=0)
    column = jnp.full(places.shape, NABOVE, jnp.int32)
    for a in range(NABOVE):
        column = jnp.where((places >> 2) == list_ref[a, group], a ^ (core * HALF), column)
    row = lax.broadcasted_iota(jnp.int32, places.shape, 0)
    table_ref[...] = column * SIDE + row * BLOCK + (places & 3) * STRIP


def pick_strips(slots, lists, strips):
    return pl.pallas_call(
        pick_kernel,
        out_shape=(
            jax.ShapeDtypeStruct((8 * HALF * STRIP, BLOCK), BF16),
            jax.ShapeDtypeStruct((HALF, 64), jnp.int32),
        ),
        in_specs=[HBM, HBM, HBM],
        out_specs=(VMEM, VMEM),
        scratch_shapes=[
            pltpu.SMEM((NABOVE, 64), jnp.int32),
            pltpu.SMEM((NABOVE, 64), jnp.int32),
            pltpu.VMEM((NABOVE, 64), jnp.int32),
            pltpu.VMEM((NABOVE * STRIP, BLOCK), BF16),
            pltpu.SemaphoreType.DMA((4,)),
        ],
        compiler_params=params(4),
        cost_estimate=cost(0, 1 << 20),
        name="pick_strips",
    )(*(pltpu.with_memory_space_constraint(x, pltpu.HBM) for x in (slots, lists, strips)))


def blocks_kernel(mine_ref, other_ref, after_ref, hi_ref, lo_ref, low_ref):
    core = lax.axis_index("panel")
    low_ref[pl.ds(pl.multiple_of(core * ROWS, ROWS), ROWS), :] = mine_ref[...]
    low_ref[pl.ds(pl.multiple_of((1 - core) * ROWS, ROWS), ROWS), :] = other_ref[...]
    row = lax.broadcasted_iota(jnp.int32, (BLOCK, BLOCK), 0)
    col = lax.broadcasted_iota(jnp.int32, (BLOCK, BLOCK), 1)
    differ = row ^ col
    below = row > col
    factors, inverses = [], []
    for b in range(8):
        at = slice(b * BLOCK, (b + 1) * BLOCK)
        factor = low_ref[at, at].astype(F32)
        diag = jnp.where(row == col, factor, 0.0)
        by_row = 1.0 / jnp.sum(diag, axis=1, keepdims=True)
        by_col = 1.0 / jnp.sum(diag, axis=0, keepdims=True)
        next_to = jnp.where(below & (differ < 2), factor, 0.0)
        inverses.append(jnp.where(row == col, by_row, 0.0) - by_row * next_to * by_col)
        factors.append(factor)
    size = 2
    while size < BLOCK:
        mask = below & (differ >= size) & (differ < 2 * size)
        for b in range(8):
            hi, lo = split(inverses[b])
            corner = jnp.where(mask, factors[b], 0.0).astype(BF16)
            both = dot(corner, jnp.concatenate([hi, lo], axis=1))
            t_hi, t_lo = split(both[:, :BLOCK] + both[:, BLOCK:])
            stacked = jnp.concatenate(
                [
                    jnp.concatenate([t_hi, t_lo], axis=1),
                    jnp.concatenate([t_hi, jnp.zeros_like(t_hi)], axis=1),
                ],
                axis=0,
            )
            both = dot(jnp.concatenate([hi, lo], axis=1), stacked)
            inverses[b] = inverses[b] - (both[:, :BLOCK] + both[:, BLOCK:])
        size *= 2
    for b in range(8):
        at = slice(b * BLOCK, (b + 1) * BLOCK)
        hi_ref[at, :], lo_ref[at, :] = split(inverses[b])


def invert_blocks(mine, other, after):
    slim = jax.ShapeDtypeStruct((SIDE, BLOCK), BF16)
    return pl.pallas_call(
        blocks_kernel,
        out_shape=(
            slim,
            slim,
            jax.ShapeDtypeStruct((SIDE, SIDE), BF16),
        ),
        in_specs=[VMEM, VMEM, ANY],
        out_specs=(VMEM, VMEM, VMEM),
        compiler_params=params(12),
        cost_estimate=cost(1 << 20, 1 << 16),
        name="invert_blocks",
    )(mine, other, after)


def solve_kernel(
    hi_slim_ref, lo_slim_ref, low_ref, coupling_ref, x_ref, y_ref, z_ref, wide_ref, square_ref, hi_ref, lo_ref
):
    mine = pl.ds(pl.multiple_of(lax.axis_index("panel") * ROWS, ROWS), ROWS)
    hi_ref[...] = jnp.zeros_like(hi_ref)
    lo_ref[...] = jnp.zeros_like(lo_ref)
    for b in range(8):
        at = slice(b * BLOCK, (b + 1) * BLOCK)
        hi_ref[at, at], lo_ref[at, at] = hi_slim_ref[at, :], lo_slim_ref[at, :]
    size = BLOCK
    while size < SIDE:
        for start in range(0, SIDE, 2 * size):
            first, second = slice(start, start + size), slice(start + size, start + 2 * size)
            corner = low_ref[second, first]
            t_hi, t_lo = split(dot(corner, hi_ref[first, first]) + dot(corner, lo_ref[first, first]))
            hi, lo = hi_ref[second, second], lo_ref[second, second]
            hi_ref[second, first], lo_ref[second, first] = split(
                -(dot(hi, t_hi) + dot(hi, t_lo) + dot(lo, t_hi))
            )
        size *= 2
    tile = 256
    for n in range(0, SIDE, tile):
        columns = slice(n, n + tile)
        wide_ref[:, columns] = dot(coupling_ref[:, n:], hi_ref[n:, columns]).astype(BF16)
    for n in range(0, SIDE, tile):
        columns = slice(n, n + tile)
        square_ref[:, columns] = dot_tn(hi_ref[n:, mine], hi_ref[n:, columns])


def solve(hi, lo, low, coupling, after):
    return pl.pallas_call(
        solve_kernel,
        out_shape=(
            jax.ShapeDtypeStruct((SIDE, SIDE), BF16),
            jax.ShapeDtypeStruct((ROWS, SIDE), F32),
        ),
        in_specs=[VMEM, VMEM, VMEM, VMEM, ANY, ANY, ANY],
        out_specs=(VMEM, VMEM),
        scratch_shapes=[pltpu.VMEM((SIDE, SIDE), BF16)] * 2,
        compiler_params=params(20),
        cost_estimate=cost(1 << 20, 1 << 16),
        name="solve",
    )(hi, lo, low, coupling, *after)


def turn_kernel(list_ref, mine_ref, other_ref, out_ref):
    core, group = lax.axis_index("panel"), lax.axis_index("front")
    out_ref[...] = jnp.zeros_like(out_ref)
    for a in range(NABOVE):
        owner, at = a // HALF, (a % HALF) * BLOCK
        row = list_ref[a, group] - core * HALF
        columns = pl.ds(pl.multiple_of(jnp.clip(row, 0, HALF - 1) * BLOCK, BLOCK), BLOCK)
        wanted = (row >= 0) & (row < HALF) & (list_ref[a, group] >= 0)

        @pl.when(wanted & (core == owner))
        def _():
            out_ref[:, columns] = mine_ref[at : at + BLOCK, :].astype(F32).T.astype(BF16)

        @pl.when(wanted & (core != owner))
        def _():
            out_ref[:, columns] = other_ref[at : at + BLOCK, :].astype(F32).T.astype(BF16)


def turn_wide(lists, mine, other):
    return pl.pallas_call(
        turn_kernel,
        out_shape=jax.ShapeDtypeStruct((SIDE, SIDE), BF16),
        in_specs=[SMEM, VMEM, VMEM],
        out_specs=VMEM,
        compiler_params=params(12),
        cost_estimate=cost(0, 8 << 20),
        name="turn_wide",
    )(lists, mine, other)


def place_strips(table_ref, sigma_ref, strips_ref, bits, low=0, high=8):
    core, group = lax.axis_index("panel"), lax.axis_index("front")
    first, second = jnp.where(core == 0, 1, 3), jnp.where(core == 0, 3, 1)
    middle = group ^ spread(bits, second)
    start = jnp.where(first == 1, middle & 0b101010, middle ^ (3 * ((middle >> 1) & 0b010101)))

    @pl.loop(low, high)
    def _(n):
        source = start ^ spread(n, first)
        for row in range(HALF):
            to = pl.multiple_of(table_ref[row, source], STRIP)
            at = pl.multiple_of((n - low) * HALF * STRIP + row * STRIP, STRIP)
            sigma_ref[pl.ds(to, STRIP), :] = strips_ref[pl.ds(at, STRIP), :]


def sigma_kernel(list_ref, table_ref, *refs):
    strips_refs, sigma_ref = refs[:7], refs[7]
    core, group = lax.axis_index("panel"), lax.axis_index("front")
    for a in range(NABOVE):
        column = pl.multiple_of((a ^ (core * HALF)) * SIDE, SIDE)

        @pl.when(list_ref[a, group] < 0)
        def _():
            sigma_ref[pl.ds(column, SIDE), :] = jnp.zeros((SIDE, BLOCK), BF16)

    for bits in range(7):
        place_strips(table_ref, sigma_ref, strips_refs[bits], bits)


SIGMA = jax.ShapeDtypeStruct(((NABOVE + 1) * SIDE, BLOCK), BF16)


def make_sigma(lists, table, strips):
    return pl.pallas_call(
        sigma_kernel,
        out_shape=SIGMA,
        in_specs=[SMEM, SMEM] + [VMEM] * 7,
        out_specs=VMEM,
        compiler_params=params(12),
        cost_estimate=cost(0, 10 << 20),
        name="make_sigma",
    )(lists, table, *strips)


def carry_kernel(
    table_ref, sigma_in_ref, top_ref, bottom_ref, mine_ref, other_ref, turned_ref, carried_ref, send_ref, sigma_ref
):
    core = lax.axis_index("panel")
    place_strips(table_ref, sigma_ref, top_ref, 7, 0, 4)
    place_strips(table_ref, sigma_ref, bottom_ref, 7, 4, 8)

    def sigma(at):
        blocks = [sigma_ref[c * SIDE : (c + 1) * SIDE, :] for c in range(at, at + HALF)]
        return jnp.concatenate(blocks, axis=1)

    tile = 256
    for n in range(0, SIDE, tile):
        columns = slice(n, n + tile)
        carried_ref[:, columns] = (
            dot(sigma(0), mine_ref[:, columns]) + dot(sigma(HALF), other_ref[:, columns])
        ).astype(BF16)
    theirs = pl.ds(pl.multiple_of((1 - core) * ROWS, ROWS), ROWS)
    for n in range(0, SIDE, tile):
        columns = slice(n, n + tile)
        send_ref[:, columns] = dot(turned_ref[theirs, :], carried_ref[:, columns]).astype(BF16)


def carry(table, sigma, last, mine, other, turned):
    return pl.pallas_call(
        carry_kernel,
        out_shape=(
            jax.ShapeDtypeStruct((SIDE, SIDE), BF16),
            jax.ShapeDtypeStruct((ROWS, SIDE), BF16),
            SIGMA,
        ),
        in_specs=[SMEM] + [VMEM] * 6,
        out_specs=(VMEM, VMEM, VMEM),
        input_output_aliases={1: 2},
        compiler_params=params(20),
        cost_estimate=cost(5 << 29, 12 << 20),
        name="carry",
    )(table, sigma, *last, mine, other, turned)


def own_kernel(turned_ref, carried_ref, square_ref, out_ref):
    mine = pl.ds(pl.multiple_of(lax.axis_index("panel") * ROWS, ROWS), ROWS)
    tile = 256
    for n in range(0, SIDE, tile):
        columns = slice(n, n + tile)
        out_ref[:, columns] = square_ref[:, columns] + dot(turned_ref[mine, :], carried_ref[:, columns])


def own_product(turned, carried, square):
    return pl.pallas_call(
        own_kernel,
        out_shape=jax.ShapeDtypeStruct((ROWS, SIDE), F32),
        in_specs=[VMEM, VMEM, VMEM],
        out_specs=VMEM,
        compiler_params=params(12),
        cost_estimate=cost(1 << 29, 8 << 20),
        name="own_product",
    )(turned, carried, square)


def finish_kernel(own_ref, received_ref, out_ref, diag_ref):
    out_ref[...] = own_ref[...] + received_ref[...].astype(F32)
    at = lax.axis_index("panel") * ROWS + pl.program_id(0) * BLOCK
    block = out_ref[:, pl.ds(pl.multiple_of(at, BLOCK), BLOCK)]
    row = lax.broadcasted_iota(jnp.int32, (BLOCK, BLOCK), 0)
    col = lax.broadcasted_iota(jnp.int32, (BLOCK, BLOCK), 1)
    diag_ref[...] = jnp.sum(jnp.where(row == col, block, 0.0), axis=0, keepdims=True)


def finish(own, received):
    rows = pl.BlockSpec((BLOCK, SIDE), lambda t: (t, 0))
    return pl.pallas_call(
        finish_kernel,
        grid=(ROWS // BLOCK,),
        out_shape=(
            jax.ShapeDtypeStruct((ROWS, SIDE), F32),
            jax.ShapeDtypeStruct((1, ROWS), F32),
        ),
        in_specs=[rows, rows],
        out_specs=(rows, pl.BlockSpec((1, BLOCK), lambda t: (0, t))),
        compiler_params=params(6),
        cost_estimate=cost(0, 6 << 20),
        name="finish",
    )(own, received)


def swap(x):
    return lax.ppermute(x, "panel", [(0, 1), (1, 0)])


def on_device(sep_factor, coup_factor, coup_list, slot_tiles, anc_tiles):
    lists, slots = coup_list.T, slot_tiles.T
    sep_other = swap(sep_factor)
    picked, table = pick_strips(slots, lists, anc_tiles)
    near = gather_cube(picked, 0)
    hi, lo, low = invert_blocks(sep_factor, sep_other, near)
    x, y, z = across(near, 1), across(near, 2), across(near, 4)
    x, y, z, hi = lax.optimization_barrier((x, y, z, hi))
    xy, yz, zx = across(x, 2), across(y, 4), across(z, 1)
    wide_mine, square = solve(hi, lo, low, coup_factor, (x, y, z))
    xy, yz, zx, wide_mine, square = lax.optimization_barrier((xy, yz, zx, wide_mine, square))
    wide_other = swap(wide_mine)
    turned = turn_wide(lists, wide_mine, wide_other)
    sigma = make_sigma(lists, table, (near, x, y, xy, z, zx, yz))
    carried, to_send, _ = carry(table, sigma, (across(xy[:SIDE], 4), across(zx[SIDE:], 2)), wide_mine, wide_other, turned)
    received = swap(to_send)
    own = own_product(turned, carried, square)
    selected, variances = finish(own, received)
    return selected, variances.reshape(ROWS)


def solution(mesh):
    placed = (P(AXES, None), P(AXES, None), P(), P(), P("front", None))
    return jax.shard_map(
        on_device,
        mesh=mesh,
        in_specs=placed,
        out_specs=(P(AXES, None), P(AXES)),
        check_vma=False,
    )
```

```python
import jax
import jax.numpy as jnp
import numpy as np
from jax import lax
from jax.experimental import pallas as pl
from jax.experimental.pallas import tpu as pltpu
from jax.sharding import PartitionSpec as P

AXES = ("front", "panel")
BLOCK = 128
STRIP = 32
NABOVE = 16
HALF = NABOVE // 2
SIDE = 1024
ROWS = SIDE // 2
F32 = jnp.float32
BF16 = jnp.bfloat16
VMEM = pl.BlockSpec(memory_space=pltpu.VMEM)
HBM = pl.BlockSpec(memory_space=pltpu.HBM)
ANY = pl.BlockSpec(memory_space=pl.ANY)
SMEM = pl.BlockSpec(memory_space=pltpu.SMEM)
MIB = 1024 * 1024


def params(mib):
    return pltpu.CompilerParams(vmem_limit_bytes=mib * MIB)


def cost(macs, moved):
    return pl.CostEstimate(flops=2 * macs, bytes_accessed=moved, transcendentals=0)


def dot(a, b):
    return jnp.dot(a, b, preferred_element_type=F32)


def dot_tn(a, b):
    return lax.dot_general(a, b, (((0,), (0,)), ((), ())), preferred_element_type=F32)


def split(x):
    hi = x.astype(BF16)
    return hi, (x - hi.astype(F32)).astype(BF16)


def spread(bits, step):
    return step * ((((bits >> 2) & 1) << 4) | (((bits >> 1) & 1) << 2) | (bits & 1))


def steps_of(core):
    return ((1, 3), (3, 1))[core]


def lowest(group, step):
    if step == 1:
        return group & 0b101010
    return group ^ (3 * ((group >> 1) & 0b010101))


def cubes(phase):
    out = []
    for core in range(2):
        step = steps_of(core)[phase]
        for first in range(64):
            if lowest(first, step) == first:
                out.append([(first ^ spread(bits, step)) * 2 + core for bits in range(8)])
    return out


def gather_cube(parts, phase):
    return lax.all_to_all(
        parts, AXES, split_axis=0, concat_axis=0, tiled=True, axis_index_groups=cubes(phase)
    )


def across(x, bits):
    pairs = []
    for group in range(64):
        for core in range(2):
            step = steps_of(core)[1]
            pairs.append((group * 2 + core, (group ^ spread(bits, step)) * 2 + core))
    return lax.ppermute(x, AXES, pairs)


def pick_kernel(slots_hbm, lists_hbm, strips_hbm, out_ref, table_ref, slots_ref, list_ref, ids_ref, held_ref, sems):
    core, group = lax.axis_index("panel"), lax.axis_index("front")
    fetches = [
        pltpu.make_async_copy(slots_hbm, slots_ref, sems.at[0]),
        pltpu.make_async_copy(strips_hbm, held_ref, sems.at[1]),
        pltpu.make_async_copy(lists_hbm, list_ref, sems.at[2]),
        pltpu.make_async_copy(slots_hbm, ids_ref, sems.at[3]),
    ]
    for fetch in fetches:
        fetch.start()
    for fetch in fetches:
        fetch.wait()
    for slot in range(NABOVE):
        row = slots_ref[slot, group] // 64 - core * HALF

        @pl.when((row >= 0) & (row < HALF))
        def _():
            strip = held_ref[slot * STRIP : (slot + 1) * STRIP, :]
            for copy in range(8):
                at = pl.multiple_of(copy * HALF * STRIP + row * STRIP, STRIP)
                out_ref[pl.ds(at, STRIP), :] = strip

    ids = ids_ref[...]
    rows = [
        jnp.sum(jnp.where((ids >> 6) == core * HALF + row, ids & 63, 0), axis=0, keepdims=True)
        for row in range(HALF)
    ]
    places = jnp.concatenate(rows, axis=0)
    column = jnp.full(places.shape, NABOVE, jnp.int32)
    for a in range(NABOVE):
        column = jnp.where((places >> 2) == list_ref[a, group], a ^ (core * HALF), column)
    row = lax.broadcasted_iota(jnp.int32, places.shape, 0)
    table_ref[...] = column * SIDE + row * BLOCK + (places & 3) * STRIP


def pick_strips(slots, lists, strips):
    return pl.pallas_call(
        pick_kernel,
        out_shape=(
            jax.ShapeDtypeStruct((8 * HALF * STRIP, BLOCK), BF16),
            jax.ShapeDtypeStruct((HALF, 64), jnp.int32),
        ),
        in_specs=[HBM, HBM, HBM],
        out_specs=(VMEM, VMEM),
        scratch_shapes=[
            pltpu.SMEM((NABOVE, 64), jnp.int32),
            pltpu.SMEM((NABOVE, 64), jnp.int32),
            pltpu.VMEM((NABOVE, 64), jnp.int32),
            pltpu.VMEM((NABOVE * STRIP, BLOCK), BF16),
            pltpu.SemaphoreType.DMA((4,)),
        ],
        compiler_params=params(4),
        cost_estimate=cost(0, 1 << 20),
        name="pick_strips",
    )(*(pltpu.with_memory_space_constraint(x, pltpu.HBM) for x in (slots, lists, strips)))


def blocks_kernel(mine_ref, other_ref, after_ref, hi_ref, lo_ref, low_ref):
    core = lax.axis_index("panel")
    low_ref[pl.ds(pl.multiple_of(core * ROWS, ROWS), ROWS), :] = mine_ref[...]
    low_ref[pl.ds(pl.multiple_of((1 - core) * ROWS, ROWS), ROWS), :] = other_ref[...]
    row = lax.broadcasted_iota(jnp.int32, (BLOCK, BLOCK), 0)
    col = lax.broadcasted_iota(jnp.int32, (BLOCK, BLOCK), 1)
    differ = row ^ col
    below = row > col
    factors, inverses = [], []
    for b in range(8):
        at = slice(b * BLOCK, (b + 1) * BLOCK)
        factor = low_ref[at, at].astype(F32)
        diag = jnp.where(row == col, factor, 0.0)
        by_row = 1.0 / jnp.sum(diag, axis=1, keepdims=True)
        by_col = 1.0 / jnp.sum(diag, axis=0, keepdims=True)
        next_to = jnp.where(below & (differ < 2), factor, 0.0)
        inverses.append(jnp.where(row == col, by_row, 0.0) - by_row * next_to * by_col)
        factors.append(factor)
    size = 2
    while size < BLOCK:
        mask = below & (differ >= size) & (differ < 2 * size)
        for b in range(8):
            hi, lo = split(inverses[b])
            corner = jnp.where(mask, factors[b], 0.0).astype(BF16)
            both = dot(corner, jnp.concatenate([hi, lo], axis=1))
            t_hi, t_lo = split(both[:, :BLOCK] + both[:, BLOCK:])
            stacked = jnp.concatenate(
                [
                    jnp.concatenate([t_hi, t_lo], axis=1),
                    jnp.concatenate([t_hi, jnp.zeros_like(t_hi)], axis=1),
                ],
                axis=0,
            )
            both = dot(jnp.concatenate([hi, lo], axis=1), stacked)
            inverses[b] = inverses[b] - (both[:, :BLOCK] + both[:, BLOCK:])
        size *= 2
    for b in range(8):
        at = slice(b * BLOCK, (b + 1) * BLOCK)
        hi_ref[at, :], lo_ref[at, :] = split(inverses[b])


def invert_blocks(mine, other, after):
    slim = jax.ShapeDtypeStruct((SIDE, BLOCK), BF16)
    return pl.pallas_call(
        blocks_kernel,
        out_shape=(
            slim,
            slim,
            jax.ShapeDtypeStruct((SIDE, SIDE), BF16),
        ),
        in_specs=[VMEM, VMEM, ANY],
        out_specs=(VMEM, VMEM, VMEM),
        compiler_params=params(12),
        cost_estimate=cost(1 << 20, 1 << 16),
        name="invert_blocks",
    )(mine, other, after)


def solve_kernel(
    hi_slim_ref, lo_slim_ref, low_ref, coupling_ref, x_ref, y_ref, z_ref, wide_ref, square_ref, hi_ref, lo_ref
):
    mine = pl.ds(pl.multiple_of(lax.axis_index("panel") * ROWS, ROWS), ROWS)
    hi_ref[...] = jnp.zeros_like(hi_ref)
    lo_ref[...] = jnp.zeros_like(lo_ref)
    for b in range(8):
        at = slice(b * BLOCK, (b + 1) * BLOCK)
        hi_ref[at, at], lo_ref[at, at] = hi_slim_ref[at, :], lo_slim_ref[at, :]
    size = BLOCK
    while size < SIDE:
        for start in range(0, SIDE, 2 * size):
            first, second = slice(start, start + size), slice(start + size, start + 2 * size)
            corner = low_ref[second, first]
            t_hi, t_lo = split(dot(corner, hi_ref[first, first]) + dot(corner, lo_ref[first, first]))
            hi, lo = hi_ref[second, second], lo_ref[second, second]
            hi_ref[second, first], lo_ref[second, first] = split(
                -(dot(hi, t_hi) + dot(hi, t_lo) + dot(lo, t_hi))
            )
        size *= 2
    tile = 256
    for n in range(0, SIDE, tile):
        columns = slice(n, n + tile)
        wide_ref[:, columns] = dot(coupling_ref[:, n:], hi_ref[n:, columns]).astype(BF16)
    for n in range(0, SIDE, tile):
        columns = slice(n, n + tile)
        square_ref[:, columns] = dot_tn(hi_ref[n:, mine], hi_ref[n:, columns])


def solve(hi, lo, low, coupling, after):
    return pl.pallas_call(
        solve_kernel,
        out_shape=(
            jax.ShapeDtypeStruct((SIDE, SIDE), BF16),
            jax.ShapeDtypeStruct((ROWS, SIDE), F32),
        ),
        in_specs=[VMEM, VMEM, VMEM, VMEM, ANY, ANY, ANY],
        out_specs=(VMEM, VMEM),
        scratch_shapes=[pltpu.VMEM((SIDE, SIDE), BF16)] * 2,
        compiler_params=params(20),
        cost_estimate=cost(1 << 20, 1 << 16),
        name="solve",
    )(hi, lo, low, coupling, *after)


def turn_kernel(list_ref, mine_ref, other_ref, out_ref):
    core, group = lax.axis_index("panel"), lax.axis_index("front")
    out_ref[...] = jnp.zeros_like(out_ref)
    for a in range(NABOVE):
        owner, at = a // HALF, (a % HALF) * BLOCK
        row = list_ref[a, group] - core * HALF
        columns = pl.ds(pl.multiple_of(jnp.clip(row, 0, HALF - 1) * BLOCK, BLOCK), BLOCK)
        wanted = (row >= 0) & (row < HALF) & (list_ref[a, group] >= 0)

        @pl.when(wanted & (core == owner))
        def _():
            out_ref[:, columns] = mine_ref[at : at + BLOCK, :].astype(F32).T.astype(BF16)

        @pl.when(wanted & (core != owner))
        def _():
            out_ref[:, columns] = other_ref[at : at + BLOCK, :].astype(F32).T.astype(BF16)


def turn_wide(lists, mine, other):
    return pl.pallas_call(
        turn_kernel,
        out_shape=jax.ShapeDtypeStruct((SIDE, SIDE), BF16),
        in_specs=[SMEM, VMEM, VMEM],
        out_specs=VMEM,
        compiler_params=params(12),
        cost_estimate=cost(0, 8 << 20),
        name="turn_wide",
    )(lists, mine, other)


def place_strips(table_ref, sigma_ref, strips_ref, bits, low=0, high=8):
    core, group = lax.axis_index("panel"), lax.axis_index("front")
    first, second = jnp.where(core == 0, 1, 3), jnp.where(core == 0, 3, 1)
    middle = group ^ spread(bits, second)
    start = jnp.where(first == 1, middle & 0b101010, middle ^ (3 * ((middle >> 1) & 0b010101)))

    @pl.loop(low, high)
    def _(n):
        source = start ^ spread(n, first)
        for row in range(HALF):
            to = pl.multiple_of(table_ref[row, source], STRIP)
            at = pl.multiple_of((n - low) * HALF * STRIP + row * STRIP, STRIP)
            sigma_ref[pl.ds(to, STRIP), :] = strips_ref[pl.ds(at, STRIP), :]


def sigma_kernel(list_ref, table_ref, *refs):
    strips_refs, sigma_ref = refs[:4], refs[4]
    core, group = lax.axis_index("panel"), lax.axis_index("front")
    for a in range(NABOVE):
        column = pl.multiple_of((a ^ (core * HALF)) * SIDE, SIDE)

        @pl.when(list_ref[a, group] < 0)
        def _():
            sigma_ref[pl.ds(column, SIDE), :] = jnp.zeros((SIDE, BLOCK), BF16)

    for bits, strips_ref in zip((0, 1, 2, 4), strips_refs):
        place_strips(table_ref, sigma_ref, strips_ref, bits)


def more_kernel(table_ref, sigma_in_ref, xy_ref, zx_ref, yz_ref, sigma_ref):
    for bits, strips_ref in zip((3, 5, 6), (xy_ref, zx_ref, yz_ref)):
        place_strips(table_ref, sigma_ref, strips_ref, bits)


SIGMA = jax.ShapeDtypeStruct(((NABOVE + 1) * SIDE, BLOCK), BF16)


def make_sigma(lists, table, strips):
    return pl.pallas_call(
        sigma_kernel,
        out_shape=SIGMA,
        in_specs=[SMEM, SMEM] + [VMEM] * 4,
        out_specs=VMEM,
        compiler_params=params(12),
        cost_estimate=cost(1 << 20, 1 << 16),
        name="make_sigma",
    )(lists, table, *strips)


def more_sigma(table, sigma, strips):
    return pl.pallas_call(
        more_kernel,
        out_shape=SIGMA,
        in_specs=[SMEM] + [VMEM] * 4,
        out_specs=VMEM,
        input_output_aliases={1: 0},
        compiler_params=params(12),
        cost_estimate=cost(0, 5 << 20),
        name="more_sigma",
    )(table, sigma, *strips)


def carry_kernel(
    table_ref, sigma_in_ref, top_ref, bottom_ref, mine_ref, other_ref, turned_ref, carried_ref, send_ref, sigma_ref
):
    core = lax.axis_index("panel")
    place_strips(table_ref, sigma_ref, top_ref, 7, 0, 4)
    place_strips(table_ref, sigma_ref, bottom_ref, 7, 4, 8)

    def sigma(at):
        blocks = [sigma_ref[c * SIDE : (c + 1) * SIDE, :] for c in range(at, at + HALF)]
        return jnp.concatenate(blocks, axis=1)

    tile = 256
    for n in range(0, SIDE, tile):
        columns = slice(n, n + tile)
        carried_ref[:, columns] = (
            dot(sigma(0), mine_ref[:, columns]) + dot(sigma(HALF), other_ref[:, columns])
        ).astype(BF16)
    theirs = pl.ds(pl.multiple_of((1 - core) * ROWS, ROWS), ROWS)
    for n in range(0, SIDE, tile):
        columns = slice(n, n + tile)
        send_ref[:, columns] = dot(turned_ref[theirs, :], carried_ref[:, columns]).astype(BF16)


def carry(table, sigma, last, mine, other, turned):
    return pl.pallas_call(
        carry_kernel,
        out_shape=(
            jax.ShapeDtypeStruct((SIDE, SIDE), BF16),
            jax.ShapeDtypeStruct((ROWS, SIDE), BF16),
            SIGMA,
        ),
        in_specs=[SMEM] + [VMEM] * 6,
        out_specs=(VMEM, VMEM, VMEM),
        input_output_aliases={1: 2},
        compiler_params=params(20),
        cost_estimate=cost(5 << 29, 12 << 20),
        name="carry",
    )(table, sigma, *last, mine, other, turned)


def own_kernel(turned_ref, carried_ref, square_ref, out_ref):
    mine = pl.ds(pl.multiple_of(lax.axis_index("panel") * ROWS, ROWS), ROWS)
    tile = 256
    for n in range(0, SIDE, tile):
        columns = slice(n, n + tile)
        out_ref[:, columns] = square_ref[:, columns] + dot(turned_ref[mine, :], carried_ref[:, columns])


def own_product(turned, carried, square):
    return pl.pallas_call(
        own_kernel,
        out_shape=jax.ShapeDtypeStruct((ROWS, SIDE), F32),
        in_specs=[VMEM, VMEM, VMEM],
        out_specs=VMEM,
        compiler_params=params(12),
        cost_estimate=cost(1 << 29, 8 << 20),
        name="own_product",
    )(turned, carried, square)


def finish_kernel(own_ref, received_ref, out_ref, diag_ref):
    out_ref[...] = own_ref[...] + received_ref[...].astype(F32)
    at = lax.axis_index("panel") * ROWS + pl.program_id(0) * BLOCK
    block = out_ref[:, pl.ds(pl.multiple_of(at, BLOCK), BLOCK)]
    row = lax.broadcasted_iota(jnp.int32, (BLOCK, BLOCK), 0)
    col = lax.broadcasted_iota(jnp.int32, (BLOCK, BLOCK), 1)
    diag_ref[...] = jnp.sum(jnp.where(row == col, block, 0.0), axis=0, keepdims=True)


def finish(own, received):
    rows = pl.BlockSpec((BLOCK, SIDE), lambda t: (t, 0))
    return pl.pallas_call(
        finish_kernel,
        grid=(ROWS // BLOCK,),
        out_shape=(
            jax.ShapeDtypeStruct((ROWS, SIDE), F32),
            jax.ShapeDtypeStruct((1, ROWS), F32),
        ),
        in_specs=[rows, rows],
        out_specs=(rows, pl.BlockSpec((1, BLOCK), lambda t: (0, t))),
        compiler_params=params(6),
        cost_estimate=cost(0, 6 << 20),
        name="finish",
    )(own, received)


def swap(x):
    return lax.ppermute(x, "panel", [(0, 1), (1, 0)])


def on_device(sep_factor, coup_factor, coup_list, slot_tiles, anc_tiles):
    lists, slots = coup_list.T, slot_tiles.T
    sep_other = swap(sep_factor)
    picked, table = pick_strips(slots, lists, anc_tiles)
    near = gather_cube(picked, 0)
    hi, lo, low = invert_blocks(sep_factor, sep_other, near)
    x, y, z = across(near, 1), across(near, 2), across(near, 4)
    x, y, z, hi = lax.optimization_barrier((x, y, z, hi))
    xy, yz, zx = across(x, 2), across(y, 4), across(z, 1)
    wide_mine, square = solve(hi, lo, low, coup_factor, (x, y, z))
    sigma = make_sigma(lists, table, (near, x, y, z))
    xy, yz, zx, wide_mine, square, sigma = lax.optimization_barrier((xy, yz, zx, wide_mine, square, sigma))
    wide_other = swap(wide_mine)
    turned = turn_wide(lists, wide_mine, wide_other)
    sigma = more_sigma(table, sigma, (xy, zx, yz))
    carried, to_send, _ = carry(table, sigma, (across(xy[:SIDE], 4), across(zx[SIDE:], 2)), wide_mine, wide_other, turned)
    received = swap(to_send)
    own = own_product(turned, carried, square)
    selected, variances = finish(own, received)
    return selected, variances.reshape(ROWS)


def solution(mesh):
    placed = (P(AXES, None), P(AXES, None), P(), P(), P("front", None))
    return jax.shard_map(
        on_device,
        mesh=mesh,
        in_specs=placed,
        out_specs=(P(AXES, None), P(AXES)),
        check_vma=False,
    )
```

```python
import jax
import jax.numpy as jnp
import numpy as np
from jax import lax
from jax.experimental import pallas as pl
from jax.experimental.pallas import tpu as pltpu
from jax.sharding import PartitionSpec as P

AXES = ("front", "panel")
BLOCK = 128
STRIP = 32
NABOVE = 16
HALF = NABOVE // 2
SIDE = 1024
ROWS = SIDE // 2
F32 = jnp.float32
BF16 = jnp.bfloat16
VMEM = pl.BlockSpec(memory_space=pltpu.VMEM)
HBM = pl.BlockSpec(memory_space=pltpu.HBM)
ANY = pl.BlockSpec(memory_space=pl.ANY)
SMEM = pl.BlockSpec(memory_space=pltpu.SMEM)
MIB = 1024 * 1024


def params(mib):
    return pltpu.CompilerParams(vmem_limit_bytes=mib * MIB)


def cost(macs, moved):
    return pl.CostEstimate(flops=2 * macs, bytes_accessed=moved, transcendentals=0)


def dot(a, b):
    return jnp.dot(a, b, preferred_element_type=F32)


def dot_tn(a, b):
    return lax.dot_general(a, b, (((0,), (0,)), ((), ())), preferred_element_type=F32)


def split(x):
    hi = x.astype(BF16)
    return hi, (x - hi.astype(F32)).astype(BF16)


def spread(bits, step):
    return step * ((((bits >> 2) & 1) << 4) | (((bits >> 1) & 1) << 2) | (bits & 1))


def steps_of(core):
    return ((1, 3), (3, 1))[core]


def lowest(group, step):
    if step == 1:
        return group & 0b101010
    return group ^ (3 * ((group >> 1) & 0b010101))


def cubes(phase):
    out = []
    for core in range(2):
        step = steps_of(core)[phase]
        for first in range(64):
            if lowest(first, step) == first:
                out.append([(first ^ spread(bits, step)) * 2 + core for bits in range(8)])
    return out


def gather_cube(parts, phase):
    return lax.all_to_all(
        parts, AXES, split_axis=0, concat_axis=0, tiled=True, axis_index_groups=cubes(phase)
    )


def across(x, bits):
    pairs = []
    for group in range(64):
        for core in range(2):
            step = steps_of(core)[1]
            pairs.append((group * 2 + core, (group ^ spread(bits, step)) * 2 + core))
    return lax.ppermute(x, AXES, pairs)


def pick_kernel(slots_hbm, lists_hbm, strips_hbm, out_ref, table_ref, slots_ref, list_ref, ids_ref, held_ref, sems):
    core, group = lax.axis_index("panel"), lax.axis_index("front")
    fetches = [
        pltpu.make_async_copy(slots_hbm, slots_ref, sems.at[0]),
        pltpu.make_async_copy(strips_hbm, held_ref, sems.at[1]),
        pltpu.make_async_copy(lists_hbm, list_ref, sems.at[2]),
        pltpu.make_async_copy(slots_hbm, ids_ref, sems.at[3]),
    ]
    for fetch in fetches:
        fetch.start()
    for fetch in fetches:
        fetch.wait()
    for slot in range(NABOVE):
        row = slots_ref[slot, group] // 64 - core * HALF

        @pl.when((row >= 0) & (row < HALF))
        def _():
            strip = held_ref[slot * STRIP : (slot + 1) * STRIP, :]
            for copy in range(8):
                at = pl.multiple_of(copy * HALF * STRIP + row * STRIP, STRIP)
                out_ref[pl.ds(at, STRIP), :] = strip

    ids = ids_ref[...]
    rows = [
        jnp.sum(jnp.where((ids >> 6) == core * HALF + row, ids & 63, 0), axis=0, keepdims=True)
        for row in range(HALF)
    ]
    places = jnp.concatenate(rows, axis=0)
    column = jnp.full(places.shape, NABOVE, jnp.int32)
    for a in range(NABOVE):
        column = jnp.where((places >> 2) == list_ref[a, group], a ^ (core * HALF), column)
    row = lax.broadcasted_iota(jnp.int32, places.shape, 0)
    table_ref[...] = column * SIDE + row * BLOCK + (places & 3) * STRIP


def pick_strips(slots, lists, strips):
    return pl.pallas_call(
        pick_kernel,
        out_shape=(
            jax.ShapeDtypeStruct((8 * HALF * STRIP, BLOCK), BF16),
            jax.ShapeDtypeStruct((HALF, 64), jnp.int32),
        ),
        in_specs=[HBM, HBM, HBM],
        out_specs=(VMEM, VMEM),
        scratch_shapes=[
            pltpu.SMEM((NABOVE, 64), jnp.int32),
            pltpu.SMEM((NABOVE, 64), jnp.int32),
            pltpu.VMEM((NABOVE, 64), jnp.int32),
            pltpu.VMEM((NABOVE * STRIP, BLOCK), BF16),
            pltpu.SemaphoreType.DMA((4,)),
        ],
        compiler_params=params(4),
        cost_estimate=cost(0, 1 << 20),
        name="pick_strips",
    )(*(pltpu.with_memory_space_constraint(x, pltpu.HBM) for x in (slots, lists, strips)))


def blocks_kernel(mine_ref, other_ref, after_ref, hi_ref, lo_ref, low_ref):
    core = lax.axis_index("panel")
    low_ref[pl.ds(pl.multiple_of(core * ROWS, ROWS), ROWS), :] = mine_ref[...]
    low_ref[pl.ds(pl.multiple_of((1 - core) * ROWS, ROWS), ROWS), :] = other_ref[...]
    row = lax.broadcasted_iota(jnp.int32, (BLOCK, BLOCK), 0)
    col = lax.broadcasted_iota(jnp.int32, (BLOCK, BLOCK), 1)
    differ = row ^ col
    below = row > col
    factors, inverses = [], []
    for b in range(8):
        at = slice(b * BLOCK, (b + 1) * BLOCK)
        factor = low_ref[at, at].astype(F32)
        diag = jnp.where(row == col, factor, 0.0)
        by_row = 1.0 / jnp.sum(diag, axis=1, keepdims=True)
        by_col = 1.0 / jnp.sum(diag, axis=0, keepdims=True)
        next_to = jnp.where(below & (differ < 2), factor, 0.0)
        inverses.append(jnp.where(row == col, by_row, 0.0) - by_row * next_to * by_col)
        factors.append(factor)
    size = 2
    while size < BLOCK:
        mask = below & (differ >= size) & (differ < 2 * size)
        for b in range(8):
            hi, lo = split(inverses[b])
            corner = jnp.where(mask, factors[b], 0.0).astype(BF16)
            both = dot(corner, jnp.concatenate([hi, lo], axis=1))
            t_hi, t_lo = split(both[:, :BLOCK] + both[:, BLOCK:])
            stacked = jnp.concatenate(
                [
                    jnp.concatenate([t_hi, t_lo], axis=1),
                    jnp.concatenate([t_hi, jnp.zeros_like(t_hi)], axis=1),
                ],
                axis=0,
            )
            both = dot(jnp.concatenate([hi, lo], axis=1), stacked)
            inverses[b] = inverses[b] - (both[:, :BLOCK] + both[:, BLOCK:])
        size *= 2
    for b in range(8):
        at = slice(b * BLOCK, (b + 1) * BLOCK)
        hi_ref[at, :], lo_ref[at, :] = split(inverses[b])


def invert_blocks(mine, other, after):
    slim = jax.ShapeDtypeStruct((SIDE, BLOCK), BF16)
    return pl.pallas_call(
        blocks_kernel,
        out_shape=(
            slim,
            slim,
            jax.ShapeDtypeStruct((SIDE, SIDE), BF16),
        ),
        in_specs=[VMEM, VMEM, ANY],
        out_specs=(VMEM, VMEM, VMEM),
        compiler_params=params(12),
        cost_estimate=cost(1 << 20, 1 << 16),
        name="invert_blocks",
    )(mine, other, after)


def solve_kernel(
    hi_slim_ref, lo_slim_ref, low_ref, coupling_ref, x_ref, y_ref, z_ref, wide_ref, square_ref, hi_ref, lo_ref
):
    mine = pl.ds(pl.multiple_of(lax.axis_index("panel") * ROWS, ROWS), ROWS)
    hi_ref[...] = jnp.zeros_like(hi_ref)
    lo_ref[...] = jnp.zeros_like(lo_ref)
    for b in range(8):
        at = slice(b * BLOCK, (b + 1) * BLOCK)
        hi_ref[at, at], lo_ref[at, at] = hi_slim_ref[at, :], lo_slim_ref[at, :]
    size = BLOCK
    while size < SIDE:
        for start in range(0, SIDE, 2 * size):
            first, second = slice(start, start + size), slice(start + size, start + 2 * size)
            corner = low_ref[second, first]
            t_hi, t_lo = split(dot(corner, hi_ref[first, first]) + dot(corner, lo_ref[first, first]))
            hi, lo = hi_ref[second, second], lo_ref[second, second]
            hi_ref[second, first], lo_ref[second, first] = split(
                -(dot(hi, t_hi) + dot(hi, t_lo) + dot(lo, t_hi))
            )
        size *= 2
    tile = 256
    for n in range(0, SIDE, tile):
        columns = slice(n, n + tile)
        wide_ref[:, columns] = dot(coupling_ref[:, n:], hi_ref[n:, columns]).astype(BF16)
    for n in range(0, SIDE, tile):
        columns = slice(n, n + tile)
        square_ref[:, columns] = dot_tn(hi_ref[n:, mine], hi_ref[n:, columns])


def solve(hi, lo, low, coupling, after):
    return pl.pallas_call(
        solve_kernel,
        out_shape=(
            jax.ShapeDtypeStruct((SIDE, SIDE), BF16),
            jax.ShapeDtypeStruct((ROWS, SIDE), F32),
        ),
        in_specs=[VMEM, VMEM, VMEM, VMEM, ANY, ANY, ANY],
        out_specs=(VMEM, VMEM),
        scratch_shapes=[pltpu.VMEM((SIDE, SIDE), BF16)] * 2,
        compiler_params=params(20),
        cost_estimate=cost(1 << 20, 1 << 16),
        name="solve",
    )(hi, lo, low, coupling, *after)


def turn_kernel(list_ref, mine_ref, other_ref, out_ref):
    core, group = lax.axis_index("panel"), lax.axis_index("front")
    out_ref[...] = jnp.zeros_like(out_ref)
    for a in range(NABOVE):
        owner, at = a // HALF, (a % HALF) * BLOCK
        row = list_ref[a, group] - core * HALF
        columns = pl.ds(pl.multiple_of(jnp.clip(row, 0, HALF - 1) * BLOCK, BLOCK), BLOCK)
        wanted = (row >= 0) & (row < HALF) & (list_ref[a, group] >= 0)

        @pl.when(wanted & (core == owner))
        def _():
            out_ref[:, columns] = mine_ref[at : at + BLOCK, :].astype(F32).T.astype(BF16)

        @pl.when(wanted & (core != owner))
        def _():
            out_ref[:, columns] = other_ref[at : at + BLOCK, :].astype(F32).T.astype(BF16)


def turn_wide(lists, mine, other):
    return pl.pallas_call(
        turn_kernel,
        out_shape=jax.ShapeDtypeStruct((SIDE, SIDE), BF16),
        in_specs=[SMEM, VMEM, VMEM],
        out_specs=VMEM,
        compiler_params=params(12),
        cost_estimate=cost(0, 8 << 20),
        name="turn_wide",
    )(lists, mine, other)


def place_strips(table_ref, sigma_ref, strips_ref, bits, low=0, high=8):
    core, group = lax.axis_index("panel"), lax.axis_index("front")
    first, second = jnp.where(core == 0, 1, 3), jnp.where(core == 0, 3, 1)
    middle = group ^ spread(bits, second)
    start = jnp.where(first == 1, middle & 0b101010, middle ^ (3 * ((middle >> 1) & 0b010101)))

    @pl.loop(low, high)
    def _(n):
        source = start ^ spread(n, first)
        for row in range(HALF):
            to = pl.multiple_of(table_ref[row, source], STRIP)
            at = pl.multiple_of((n - low) * HALF * STRIP + row * STRIP, STRIP)
            sigma_ref[pl.ds(to, STRIP), :] = strips_ref[pl.ds(at, STRIP), :]


def sigma_kernel(list_ref, table_ref, *refs):
    strips_refs, sigma_ref = refs[:7], refs[7]
    core, group = lax.axis_index("panel"), lax.axis_index("front")
    for a in range(NABOVE):
        column = pl.multiple_of((a ^ (core * HALF)) * SIDE, SIDE)

        @pl.when(list_ref[a, group] < 0)
        def _():
            sigma_ref[pl.ds(column, SIDE), :] = jnp.zeros((SIDE, BLOCK), BF16)

    for bits in range(7):
        place_strips(table_ref, sigma_ref, strips_refs[bits], bits)


SIGMA = jax.ShapeDtypeStruct(((NABOVE + 1) * SIDE, BLOCK), BF16)


def make_sigma(lists, table, strips):
    return pl.pallas_call(
        sigma_kernel,
        out_shape=SIGMA,
        in_specs=[SMEM, SMEM] + [VMEM] * 7,
        out_specs=VMEM,
        compiler_params=params(12),
        cost_estimate=cost(0, 10 << 20),
        name="make_sigma",
    )(lists, table, *strips)


def carry_kernel(
    table_ref, sigma_in_ref, top_ref, bottom_ref, mine_ref, other_ref, turned_ref, carried_ref, send_ref, sigma_ref
):
    core = lax.axis_index("panel")
    place_strips(table_ref, sigma_ref, top_ref, 7, 0, 4)
    place_strips(table_ref, sigma_ref, bottom_ref, 7, 4, 8)

    def sigma(at):
        blocks = [sigma_ref[c * SIDE : (c + 1) * SIDE, :] for c in range(at, at + HALF)]
        return jnp.concatenate(blocks, axis=1)

    tile = 512
    for n in range(0, SIDE, tile):
        columns = slice(n, n + tile)
        carried_ref[:, columns] = (
            dot(sigma(0), mine_ref[:, columns]) + dot(sigma(HALF), other_ref[:, columns])
        ).astype(BF16)
    theirs = pl.ds(pl.multiple_of((1 - core) * ROWS, ROWS), ROWS)
    for n in range(0, SIDE, tile):
        columns = slice(n, n + tile)
        send_ref[:, columns] = dot(turned_ref[theirs, :], carried_ref[:, columns]).astype(BF16)


def carry(table, sigma, last, mine, other, turned):
    return pl.pallas_call(
        carry_kernel,
        out_shape=(
            jax.ShapeDtypeStruct((SIDE, SIDE), BF16),
            jax.ShapeDtypeStruct((ROWS, SIDE), BF16),
            SIGMA,
        ),
        in_specs=[SMEM] + [VMEM] * 6,
        out_specs=(VMEM, VMEM, VMEM),
        input_output_aliases={1: 2},
        compiler_params=params(20),
        cost_estimate=cost(5 << 29, 12 << 20),
        name="carry",
    )(table, sigma, *last, mine, other, turned)


def own_kernel(turned_ref, carried_ref, square_ref, out_ref):
    mine = pl.ds(pl.multiple_of(lax.axis_index("panel") * ROWS, ROWS), ROWS)
    tile = 256
    for n in range(0, SIDE, tile):
        columns = slice(n, n + tile)
        out_ref[:, columns] = square_ref[:, columns] + dot(turned_ref[mine, :], carried_ref[:, columns])


def own_product(turned, carried, square):
    return pl.pallas_call(
        own_kernel,
        out_shape=jax.ShapeDtypeStruct((ROWS, SIDE), F32),
        in_specs=[VMEM, VMEM, VMEM],
        out_specs=VMEM,
        compiler_params=params(12),
        cost_estimate=cost(1 << 29, 8 << 20),
        name="own_product",
    )(turned, carried, square)


def finish_kernel(own_ref, received_ref, out_ref, diag_ref):
    out_ref[...] = own_ref[...] + received_ref[...].astype(F32)
    at = lax.axis_index("panel") * ROWS + pl.program_id(0) * BLOCK
    block = out_ref[:, pl.ds(pl.multiple_of(at, BLOCK), BLOCK)]
    row = lax.broadcasted_iota(jnp.int32, (BLOCK, BLOCK), 0)
    col = lax.broadcasted_iota(jnp.int32, (BLOCK, BLOCK), 1)
    diag_ref[...] = jnp.sum(jnp.where(row == col, block, 0.0), axis=0, keepdims=True)


def finish(own, received):
    rows = pl.BlockSpec((BLOCK, SIDE), lambda t: (t, 0))
    return pl.pallas_call(
        finish_kernel,
        grid=(ROWS // BLOCK,),
        out_shape=(
            jax.ShapeDtypeStruct((ROWS, SIDE), F32),
            jax.ShapeDtypeStruct((1, ROWS), F32),
        ),
        in_specs=[rows, rows],
        out_specs=(rows, pl.BlockSpec((1, BLOCK), lambda t: (0, t))),
        compiler_params=params(6),
        cost_estimate=cost(0, 6 << 20),
        name="finish",
    )(own, received)


def swap(x):
    return lax.ppermute(x, "panel", [(0, 1), (1, 0)])


def on_device(sep_factor, coup_factor, coup_list, slot_tiles, anc_tiles):
    lists, slots = coup_list.T, slot_tiles.T
    sep_other = swap(sep_factor)
    picked, table = pick_strips(slots, lists, anc_tiles)
    near = gather_cube(picked, 0)
    hi, lo, low = invert_blocks(sep_factor, sep_other, near)
    x, y, z = across(near, 1), across(near, 2), across(near, 4)
    x, y, z, hi = lax.optimization_barrier((x, y, z, hi))
    xy, yz, zx = across(x, 2), across(y, 4), across(z, 1)
    wide_mine, square = solve(hi, lo, low, coup_factor, (x, y, z))
    xy, yz, zx, wide_mine, square = lax.optimization_barrier((xy, yz, zx, wide_mine, square))
    wide_other = swap(wide_mine)
    turned = turn_wide(lists, wide_mine, wide_other)
    sigma = make_sigma(lists, table, (near, x, y, xy, z, zx, yz))
    carried, to_send, _ = carry(table, sigma, (across(xy[:SIDE], 4), across(zx[SIDE:], 2)), wide_mine, wide_other, turned)
    received = swap(to_send)
    own = own_product(turned, carried, square)
    selected, variances = finish(own, received)
    return selected, variances.reshape(ROWS)


def solution(mesh):
    placed = (P(AXES, None), P(AXES, None), P(), P(), P("front", None))
    return jax.shard_map(
        on_device,
        mesh=mesh,
        in_specs=placed,
        out_specs=(P(AXES, None), P(AXES)),
        check_vma=False,
    )
```
